32 devices in a mesh: patch: 2 (over x), epoch: 8 (over z, y), tile: 2 (over core).
Axes of the slice: x: 2, y: 2, z: 4, core: 2. Of those that a mesh axis runs over, the one named last changes fastest.
Arguments:
- template: float32 [1024, 1024], P(('patch', 'tile'), 'epoch'), parts along dimension 0, may hold values from -6 to 6
- science: float32 [16, 512, 1024], P(('patch', 'epoch'), 'tile'), parts along dimension 0, may hold values from -6 to 6, as said below
- flags: int32 [16, 512, 1024], P(('patch', 'epoch'), 'tile'), parts along dimension 0, may hold values 0 or 1
- stamp_rows: int32 [16, 32], P(('patch', 'epoch'), 'tile'), parts along dimension 0, may hold values from 0 to 224
- stamp_cols: int32 [16, 32], P(('patch', 'epoch'), 'tile'), parts along dimension 0, may hold values from 0 to 992
Outputs:
- detection: float32 [16, 512, 1024], P(('patch', 'epoch'), 'tile'), parts along dimension 0
- coefficients: float32 [24], P('patch'), parts along dimension 0
The draws below stay inside these ranges and needn't reach their ends.
There are 2 independent parts, one for each index of `patch`. The reference program is written for one: setup_inputs(seed, part) draws one part's arguments, and reference() takes and returns one part's arrays. A program takes and returns all parts, laid end to end along the dimension named above; each array names one. Nothing has to cross between parts.
Inputs may be any that keep to these rules, and one draw needn't show every extreme that they name: `stamp_rows`: stamps lie inside their tile. `stamp_cols`: stamps lie inside the image. `science`: each exposure is the template matched by some kernel, plus noise.
All inputs are finite; a program needn't handle non-finite values. No bound on the sum of `flags` on one device may be relied on, other than what follows from the above.
Results may differ from the reference program's by a relative error of at most 0.0003.
Values sent between devices are 32-bit elements; how exact they have to be, the bound alone decides.
No kernel may reach another device: no remote copies, remote signals or barrier semaphores. Data moves between devices by JAX's collectives and lax.ppermute only.
A program may use at most 128 MiB of HBM per device.

```python
import jax
import jax.numpy as jnp
from jax import lax

R_DEV = 256
COLS = 1024
STAMPS_DEV = 16
STAMP = 32
NBASIS = 12
ROWS = 512
EPOCHS = 8
STAMPS = 32


def draw_profiles():
    offsets = jnp.arange(15, dtype=jnp.float32) - 7.0
    row_list = []
    col_list = []
    for sigma in (1.0, 2.0, 3.5):
        gauss = jnp.exp(-offsets * offsets / (2.0 * sigma * sigma))
        gauss = gauss / jnp.sum(gauss)
        for power_r, power_c in ((0, 0), (1, 0), (0, 1), (1, 1)):
            row_list.append(gauss * (offsets / 7.0) if power_r else gauss)
            col_list.append(gauss * (offsets / 7.0) if power_c else gauss)
    return (jnp.stack(row_list), jnp.stack(col_list))


def draw_rows_conv(extended, profile):
    count = extended.shape[0] - 14
    total = jnp.zeros((profile.shape[0], count, extended.shape[1]), jnp.float32)
    for shift in range(15):
        total = total + profile[:, shift, None, None] * extended[None, shift:shift + count, :]
    return total


def draw_cols_conv(extended, profile):
    count = extended.shape[2] - 14
    total = jnp.zeros((profile.shape[0], extended.shape[1], count), jnp.float32)
    for shift in range(15):
        total = total + profile[:, shift, None, None] * extended[:, :, shift:shift + count]
    return total


def template_field(key):
    field = jax.random.normal(jax.random.fold_in(key, 101), (ROWS, COLS), jnp.float32)
    return jnp.clip(field, -6.0, 6.0)


def draw_template(key, part):
    return template_field(key)


def draw_science(key, part):
    field = template_field(key)
    row_prof, col_prof = draw_profiles()
    images = draw_cols_conv(draw_rows_conv(jnp.pad(field, 7), row_prof), col_prof)
    mixing = 0.15 * jax.random.normal(jax.random.fold_in(key, 201), (EPOCHS, 12), jnp.float32)
    mixing = mixing + jax.nn.one_hot(4, 12, dtype=jnp.float32)[None, :]
    blurred = jnp.einsum('ek,krc->erc', mixing, images, precision=lax.Precision.HIGHEST)
    noise = 0.08 * jax.random.normal(jax.random.fold_in(key, 202), (EPOCHS, ROWS, COLS), jnp.float32)
    return jnp.clip(blurred + noise, -6.0, 6.0)


def plant(array, rng, low, high):
    place = [jax.random.randint(jax.random.fold_in(rng, axis), (), 0, length) for axis, length in enumerate(array.shape)]
    main_axis = array.shape.index(max(array.shape))
    neighbour = place[:main_axis] + [(place[main_axis] + 1) % array.shape[main_axis]] + place[main_axis + 1:]
    return array.at[tuple(place)].set(low).at[tuple(neighbour)].set(high)


def setup_inputs(seed: int = 0, part: int = 0) -> dict:
    key_of = jax.random.split(jax.random.key(seed), 6)
    part_splits = jax.random.split(jax.random.fold_in(key_of[5], part), 6)
    template = draw_template(jax.random.fold_in(jax.random.fold_in(key_of[5], part), 71), part)
    science = draw_science(jax.random.fold_in(jax.random.fold_in(key_of[5], part), 71), part)
    flags = plant((jax.random.randint(part_splits[2], (EPOCHS, ROWS, COLS), 0, 16) < 1).astype(jnp.int32), jax.random.fold_in(part_splits[2], 1), 0, 1)
    stamp_rows = plant(jax.random.randint(part_splits[3], (EPOCHS, STAMPS), 0, R_DEV - STAMP + 1), jax.random.fold_in(part_splits[3], 1), 0, R_DEV - STAMP).astype(jnp.int32)
    stamp_cols = plant(jax.random.randint(part_splits[4], (EPOCHS, STAMPS), 0, COLS - STAMP + 1), jax.random.fold_in(part_splits[4], 1), 0, COLS - STAMP).astype(jnp.int32)
    return dict(template=template, science=science, flags=flags, stamp_rows=stamp_rows, stamp_cols=stamp_cols)


def basis_profiles():
    offsets = jnp.arange(15, dtype=jnp.float32) - 7.0
    row_list = []
    col_list = []
    for sigma in (1.0, 2.0, 3.5):
        gauss = jnp.exp(-offsets * offsets / (2.0 * sigma * sigma))
        gauss = gauss / jnp.sum(gauss)
        for power_r, power_c in ((0, 0), (1, 0), (0, 1), (1, 1)):
            row_list.append(gauss * (offsets / 7.0) if power_r else gauss)
            col_list.append(gauss * (offsets / 7.0) if power_c else gauss)
    return (jnp.stack(row_list), jnp.stack(col_list))

def psf_profile():
    offsets = jnp.arange(15, dtype=jnp.float32) - 7.0
    gauss = jnp.exp(-offsets * offsets / 4.5)
    return (gauss / jnp.sum(gauss))[None, :]

def conv_rows(extended, profile):
    count = extended.shape[0] - 14
    total = jnp.zeros((profile.shape[0], count, extended.shape[1]), jnp.float32)
    for shift in range(15):
        total = total + profile[:, shift, None, None] * extended[None, shift:shift + count, :]
    return total

def conv_cols(extended, profile):
    count = extended.shape[2] - 14
    total = jnp.zeros((profile.shape[0], extended.shape[1], count), jnp.float32)
    for shift in range(15):
        total = total + profile[:, shift, None, None] * extended[:, :, shift:shift + count]
    return total

def reference(template, science, flags, stamp_rows, stamp_cols):
    row_prof, col_prof = basis_profiles()
    images = conv_cols(conv_rows(jnp.pad(template, 7), row_prof), col_prof)
    tile_of = (jnp.arange(stamp_rows.shape[1]) // STAMPS_DEV).astype(jnp.int32)
    top = stamp_rows + tile_of[None, :] * R_DEV
    pos_r = jnp.arange(ROWS).astype(jnp.int32)
    pos_c = jnp.arange(COLS).astype(jnp.int32)

    def one_epoch(epoch):
        row_ind = ((pos_r[None, :] >= top[epoch][:, None]) & (pos_r[None, :] < top[epoch][:, None] + STAMP)).astype(jnp.float32)
        col_ind = ((pos_c[None, :] >= stamp_cols[epoch][:, None]) & (pos_c[None, :] < stamp_cols[epoch][:, None] + STAMP)).astype(jnp.float32)
        weight = jnp.dot(row_ind.T, col_ind, precision=lax.Precision.HIGHEST)
        good = jnp.where(flags[epoch] == 0, weight, 0.0)
        normal = jnp.einsum('kpq,lpq->kl', images * good[None], images, precision=lax.Precision.HIGHEST)
        rhs = jnp.einsum('kpq,pq->k', images, good * science[epoch], precision=lax.Precision.HIGHEST)
        return (normal, rhs)
    normals, rhss = lax.map(one_epoch, jnp.arange(science.shape[0]).astype(jnp.int32))
    normal = jnp.sum(normals, axis=0)
    rhs = jnp.sum(rhss, axis=0)
    system = normal + 0.05 * jnp.trace(normal) / NBASIS * jnp.eye(NBASIS, dtype=jnp.float32)
    coefficients = jnp.linalg.solve(system, rhs)
    model = jnp.einsum('k,kpq->pq', coefficients, images, precision=lax.Precision.HIGHEST)
    psf = psf_profile()

    def filter_one(epoch):
        difference = science[epoch] - model
        return conv_cols(conv_rows(jnp.pad(difference, 7), psf), psf)[0]
    detection = lax.map(filter_one, jnp.arange(science.shape[0]).astype(jnp.int32))
    return (detection, coefficients)
```

```python
import functools

import jax
import jax.numpy as jnp
import numpy as np
from jax import lax
from jax.experimental import pallas as pl
from jax.experimental.pallas import tpu as pltpu
from jax.sharding import PartitionSpec as P

STAMP = 32
HALF = 7
TAPS = 15
SIGMAS = (1.0, 2.0, 3.5)
NB = 12
LANES = 128
HALO = 16
WIN = LANES + 2 * HALO
PATCH_ROWS = 48
F32 = jnp.float32
BF16 = jnp.bfloat16
LIMIT = 56 * 1024 * 1024


def split_np(a):
    a = np.asarray(a, np.float32)
    hi = a.astype(BF16)
    lo = (a - hi.astype(np.float32)).astype(BF16)
    return hi, lo


def profiles():
    offsets = np.arange(TAPS, dtype=np.float64) - HALF
    rows = []
    for sigma in SIGMAS:
        gauss = np.exp(-offsets * offsets / (2.0 * sigma * sigma))
        gauss = gauss / gauss.sum()
        rows += [gauss, gauss * offsets / HALF]
    return np.stack(rows)


def psf_profile():
    offsets = np.arange(TAPS, dtype=np.float64) - HALF
    gauss = np.exp(-offsets * offsets / 4.5)
    return gauss / gauss.sum()


def band(profile, size):
    out = np.zeros((size, size))
    for shift in range(TAPS):
        out += profile[shift] * np.eye(size, k=shift - HALF)
    return out


def three_bands(size):
    psf = band(psf_profile(), size)
    return [psf @ band(p, size) for p in profiles()], psf


def pick(matrix, rows, cols):
    cols = np.asarray(cols)
    ok = (cols >= 0) & (cols < matrix.shape[1])
    out = matrix[np.asarray(rows)[:, None], np.clip(cols, 0, matrix.shape[1] - 1)[None, :]]
    return np.where(ok[None, :], out, 0.0)


def starts():
    return (0, LANES, 2 * LANES)


def row_tables():
    size = 3 * LANES
    ops, psf = three_bands(size)

    def stack(ms):
        out = []
        for start in starts():
            rows = np.arange(LANES) + start
            cols = np.arange(WIN) + start - HALO
            hi, lo = split_np(np.concatenate([pick(m, rows, cols) for m in ms], axis=0))
            out.append(np.concatenate([hi, hi, lo], axis=1))
        return np.stack(out)

    return stack(ops), stack([psf])


def column_tables():
    size = 3 * LANES
    ops, psf = three_bands(size)

    def one(matrix, start):
        lane = np.arange(LANES)
        cols = np.concatenate([start + lane, np.where(lane < 64, start + LANES + lane, start - LANES + lane)])
        return pick(matrix, np.arange(LANES) + start, cols).T

    model = []
    for start in starts():
        per = []
        for s in range(3):
            both = np.concatenate([one(ops[2 * s], start), one(ops[2 * s + 1], start)], axis=1)
            per.append(np.stack(split_np(both)))
        model.append(np.stack(per))
    return np.stack(model), np.stack([np.stack(split_np(one(psf, start))) for start in starts()])


def stamp_table():
    prof = profiles()
    out = np.zeros((256, 6, LANES))
    for q in range(4):
        for c in range(STAMP):
            for v in range(TAPS):
                out[q * 64 + c + v, :, q * STAMP + c] = prof[:, v]
    return np.stack(split_np(out.reshape(256, 6 * LANES)))


def pair_list():
    return [(k, l) for k in range(NB) for l in range(k, NB)] + [(k, NB) for k in range(NB)]


def place_tables():
    pairs = pair_list()
    first = np.zeros((2, 96, LANES), np.float32)
    left = np.zeros((16, 192), np.float32)
    for p, (k, l) in enumerate(pairs):
        first[0, p, l] = 1.0
        left[k, p] = 1.0
        if l < NB and l != k:
            first[1, p, k] = 1.0
            left[l, 96 + p] = 1.0
    return first, left


def dot(a, b):
    return jnp.dot(a, b, preferred_element_type=F32)


def split(x):
    hi = x.astype(BF16)
    lo = (x - hi.astype(F32)).astype(BF16)
    return hi, lo


def stack3(x):
    hi, lo = split(x)
    return jnp.concatenate([hi, lo, hi], axis=0)


def params(**kw):
    return pltpu.CompilerParams(vmem_limit_bytes=LIMIT, **kw)


VMEM = functools.partial(pl.BlockSpec, memory_space=pltpu.VMEM)
SMEM = functools.partial(pl.BlockSpec, memory_space=pltpu.SMEM)


def lane_index(shape):
    return lax.broadcasted_iota(jnp.int32, shape, len(shape) - 1)


def science_kernel(n_tile, info, tops, lefts, sci, edge, flags, lrow, wcol, d0, wp, sp, sb, fb, mid):
    tile = info[0]
    rows, cols = sci.shape
    nblk = cols // LANES
    nrow = rows // LANES
    for m in range(nblk):
        piece = slice(m * LANES, (m + 1) * LANES)
        e = edge[:, piece]
        sb[m, 0:HALO, :] = jnp.where(tile == 0, 0.0, e)
        sb[m, HALO : HALO + rows, :] = sci[:, piece]
        sb[m, HALO + rows :, :] = jnp.where(tile == n_tile - 1, 0.0, e)
        fb[m] = jnp.where(flags[:, piece] == 0, 1.0, 0.0)
    for b in range(nrow):
        v = variant(tile, b, n_tile, nrow)
        left = lrow[v]
        for m in range(0, nblk, 2):
            x = jnp.concatenate(
                [sb[m, b * LANES : b * LANES + WIN, :], sb[m + 1, b * LANES : b * LANES + WIN, :]], axis=1
            )
            y = dot(left, stack3(x))
            mid[m, b * LANES : (b + 1) * LANES, :] = y[:, :LANES]
            mid[m + 1, b * LANES : (b + 1) * LANES, :] = y[:, LANES:]
    lane = lane_index((rows, LANES))
    for m in range(nblk):
        v = 0 if m == 0 else (2 if m == nblk - 1 else 1)
        rim = jnp.where(lane < 64, mid[min(m + 1, nblk - 1)], mid[max(m - 1, 0)])
        hi, lo = split(jnp.concatenate([mid[m], rim], axis=1))
        d0[:, m * LANES : (m + 1) * LANES] = dot(hi, wcol[v, 0]) + dot(lo, wcol[v, 0]) + dot(hi, wcol[v, 1])
    lane = lane_index((STAMP, LANES))
    for g in range(tops.shape[1] // 4):
        w = jnp.zeros((STAMP, LANES), F32)
        s = jnp.zeros((STAMP, LANES), F32)
        for q in range(4):
            top = tops[0, g * 4 + q]
            left = lefts[0, g * 4 + q]
            blk = left // LANES
            off = left - blk * LANES
            nxt = jnp.minimum(blk + 1, nblk - 1)
            shift = lax.rem(q * STAMP - off + LANES, LANES)
            near = lane < q * STAMP - off + LANES
            here = (lane >= q * STAMP) & (lane < (q + 1) * STAMP)

            def window(ref, first):
                a = pltpu.roll(ref[blk, pl.ds(first, STAMP), :], shift, 1)
                b = pltpu.roll(ref[nxt, pl.ds(first, STAMP), :], shift, 1)
                return jnp.where(near, a, b)

            w = jnp.where(here, window(fb, top), w)
            s = jnp.where(here, window(sb, top + HALO), s)
        wp[g * STAMP : (g + 1) * STAMP, :] = w
        sp[g * STAMP : (g + 1) * STAMP, :] = w * s


def variant(tile, b, n_tile, nrow):
    v = jnp.int32(1)
    if b == 0:
        v = jnp.where(tile == 0, 0, v)
    if b == nrow - 1:
        v = jnp.where(tile == n_tile - 1, 2, v)
    return v


def assemble(info, n_tile, blocks, t):
    tile = info[0]
    rows = blocks[0].shape[0] - HALO
    for m in (0, len(blocks) + 1):
        t[m] = jnp.zeros(t.shape[1:], F32)
    for slot, block in enumerate(blocks):
        at = info[1 + slot] + 1
        e = block[rows:, :]
        t[at, 0:HALO, :] = jnp.where(tile == 0, 0.0, e)
        t[at, HALO : HALO + rows, :] = block[0:rows, :]
        t[at, HALO + rows :, :] = jnp.where(tile == n_tile - 1, 0.0, e)


def stamp_kernel(n_tile, nblk, info, tops, lefts, *refs):
    blocks = refs[:nblk]
    wp, sp, mcol, first, leftm, system, t, y, images, sums = refs[nblk:]
    assemble(info, n_tile, blocks, t)
    groups = tops.shape[1] // 4
    lane = lane_index((PATCH_ROWS, LANES))
    prof = profiles()
    xs = []
    for g in range(groups):
        halves = []
        for pair in range(2):
            parts = []
            for h in range(2):
                j = g * 4 + pair * 2 + h
                start = lefts[0, j] + (LANES - HALF)
                blk = start // LANES
                off = start - blk * LANES
                shift = lax.rem(64 * h - off + LANES, LANES)
                rows = pl.ds(tops[0, j] + (HALO - HALF), PATCH_ROWS)
                a = pltpu.roll(t[blk, rows, :], shift, 1)
                b = pltpu.roll(t[blk + 1, rows, :], shift, 1)
                parts.append(jnp.where(lane < 64 * h - off + LANES, a, b))
            halves.append(jnp.where(lane < 64, parts[0], parts[1]))
        xs.append(jnp.concatenate(halves, axis=1))
    hi, lo = split(jnp.concatenate(xs, axis=0))
    for p in range(6):
        piece = slice(p * LANES, (p + 1) * LANES)
        wh = mcol[0, :, piece]
        y[p] = dot(hi, wh) + dot(lo, wh) + dot(hi, mcol[1, :, piece])
    for s in range(3):
        gauss = prof[2 * s]
        for j in range(2):
            for g in range(groups):
                base = g * PATCH_ROWS

                def at(o):
                    return y[2 * s + j, base + HALF + o : base + HALF + o + STAMP, :]

                even = at(0) * np.float32(gauss[HALF])
                odd = None
                for d in range(1, HALF + 1):
                    up, down = at(d), at(-d)
                    even = even + (up + down) * np.float32(gauss[HALF + d])
                    term = (up - down) * np.float32(gauss[HALF + d] * d / HALF)
                    odd = term if odd is None else odd + term
                images[4 * s + 2 * j, g * STAMP : (g + 1) * STAMP, :] = even
                images[4 * s + 2 * j + 1, g * STAMP : (g + 1) * STAMP, :] = odd
    depth = groups * STAMP
    w = wp[...]
    weighted = None
    for p, (k, l) in enumerate(pair_list()):
        if l == NB:
            prod = sp[...] * images[k]
        else:
            if l == k:
                weighted = w * images[k]
            prod = weighted * images[l]
        sums[p * 8 : (p + 1) * 8, :] = jnp.sum(prod.reshape(depth // 8, 8, LANES), axis=0)
    used = len(pair_list())
    sums[used * 8 :, :] = jnp.zeros((96 * 8 - used * 8, LANES), F32)
    total = sums[pl.ds(0, 96, stride=8), :]
    for r in range(1, 8):
        total = total + sums[pl.ds(r, 96, stride=8), :]
    total = jnp.sum(total, axis=1, keepdims=True)
    spread = jnp.concatenate([total * first[0], total * first[1]], axis=0)
    system[...] = jnp.dot(leftm[...], spread, preferred_element_type=F32, precision=lax.Precision.HIGHEST)


def images_kernel(n_tile, nblk, info, *refs):
    blocks = refs[:nblk]
    lrow, wcol, out, t, rhi, rlo = refs[nblk:]
    m = pl.program_id(0)
    rows = rhi.shape[2]
    nrow = rows // LANES

    @pl.when(m == 0)
    def _():
        tile = info[0]
        assemble(info, n_tile, blocks, t)
        for b in range(nrow):
            left = lrow[variant(tile, b, n_tile, nrow)]
            for c in range(0, nblk, 2):
                x = jnp.concatenate(
                    [t[c + 1, b * LANES : b * LANES + WIN, :], t[c + 2, b * LANES : b * LANES + WIN, :]], axis=1
                )
                hi, lo = split(dot(left, stack3(x)))
                for p in range(6):
                    for h in range(2):
                        piece = (slice(p * LANES, (p + 1) * LANES), slice(h * LANES, (h + 1) * LANES))
                        rhi[c + h, p, b * LANES : (b + 1) * LANES, :] = hi[piece]
                        rlo[c + h, p, b * LANES : (b + 1) * LANES, :] = lo[piece]

    lane = lane_index((2 * rows, LANES))
    v = jnp.where(m == 0, 0, jnp.where(m == nblk - 1, 2, 1))
    after = jnp.minimum(m + 1, nblk - 1)
    before = jnp.maximum(m - 1, 0)
    for s in range(3):

        def window(ref):
            def get(i):
                return ref[i, 2 * s : 2 * s + 2].reshape(2 * rows, LANES)

            rim = jnp.where(lane < 64, get(after), get(before))
            return jnp.concatenate([get(m), rim], axis=1)

        hi, lo = window(rhi), window(rlo)
        q = dot(hi, wcol[v, s, 0]) + dot(lo, wcol[v, s, 0]) + dot(hi, wcol[v, s, 1])
        for i in range(2):
            for j in range(2):
                out[0, 4 * s + i + 2 * j] = q[i * rows : (i + 1) * rows, j * LANES : (j + 1) * LANES]


def final_kernel(system, d0, images, detection, coefficients, solved):
    @pl.when(pl.program_id(0) == 0)
    def _():
        a = system[...]
        row = lax.broadcasted_iota(jnp.int32, a.shape, 0)
        lane = lane_index(a.shape)
        diag = (row == lane) & (row < NB)
        trace = jnp.sum(jnp.sum(jnp.where(diag, a, 0.0), axis=1, keepdims=True), axis=0, keepdims=True)
        a = a + jnp.where(diag, 0.05 * trace / NB, 0.0)
        for k in range(NB):
            pivot = a[k : k + 1, :] / a[k : k + 1, k : k + 1]
            a = jnp.where(row == k, pivot, a - a[:, k : k + 1] * pivot)
        solved[...] = jnp.broadcast_to(a[:, NB : NB + 1], a.shape)
        for k in range(NB):
            coefficients[k] = solved[k, 0]

    total = d0[...]
    for k in range(NB):
        total = total - solved[k : k + 1, :] * images[0, k]
    detection[...] = total


def ring_order(count):
    return list(range(0, count, 2)) + list(range(count - 1, 0, -2))


def swap(x):
    return lax.ppermute(x, "tile", [(0, 1), (1, 0)])


def gather_ring(block, count):
    ring = ring_order(count)
    ahead = [(ring[i], ring[(i + 1) % count]) for i in range(count)]
    back = [(t, s) for s, t in ahead]
    out = [block]
    fwd = bwd = block
    for step in range(count // 2):
        fwd = lax.ppermute(fwd, "epoch", ahead)
        out.append(fwd)
        if step < count // 2 - 1:
            bwd = lax.ppermute(bwd, "epoch", back)
            out.append(bwd)
    return out


def ring_table(count):
    ring = ring_order(count)
    table = np.zeros((count, count), np.int32)
    for i, me in enumerate(ring):
        order = [me]
        for step in range(1, count // 2 + 1):
            order.append(ring[(i - step) % count])
            if step < count // 2:
                order.append(ring[(i + step) % count])
        table[me] = order
    return table


def all_sum(x, count):
    x = x + swap(x)
    if count & (count - 1):
        return lax.psum(x, "epoch")
    bit = 1
    while bit < count:
        x = x + lax.ppermute(x, "epoch", [(i, i ^ bit) for i in range(count)])
        bit *= 2
    return x


def local(template, science, flags, stamp_rows, stamp_cols):
    n_tile = lax.axis_size("tile")
    n_epoch = lax.axis_size("epoch")
    rows, width = template.shape
    science, flags = science[0], flags[0]
    cols = science.shape[1]
    nblk = cols // LANES
    groups = stamp_rows.shape[1] // 4
    tile = lax.axis_index("tile")

    def edge_of(x):
        return jnp.where(tile == 0, x[-HALO:], x[:HALO])

    edges = swap(jnp.concatenate([edge_of(template), edge_of(science)], axis=1))
    tall = jnp.concatenate([template, edges[:, :width]], axis=0)
    if width == LANES:
        blocks = gather_ring(tall, n_epoch)
        order = jnp.asarray(ring_table(n_epoch))[lax.axis_index("epoch")]
    else:
        whole = lax.all_gather(tall, "epoch", axis=1, tiled=True)
        blocks = [whole[:, m * LANES : (m + 1) * LANES] for m in range(nblk)]
        order = jnp.arange(nblk, dtype=jnp.int32)
    info = jnp.concatenate([tile[None].astype(jnp.int32), order])

    lrow6, lrow1 = row_tables()
    wcol6, wcol1 = column_tables()

    depth = groups * STAMP
    d0, wp, sp = pl.pallas_call(
        functools.partial(science_kernel, n_tile),
        out_shape=(
            jax.ShapeDtypeStruct((rows, cols), F32),
            jax.ShapeDtypeStruct((depth, LANES), F32),
            jax.ShapeDtypeStruct((depth, LANES), F32),
        ),
        in_specs=[SMEM()] * 3 + [VMEM()] * 5,
        out_specs=(VMEM(), VMEM(), VMEM()),
        scratch_shapes=[
            pltpu.VMEM((nblk, rows + 2 * HALO, LANES), F32),
            pltpu.VMEM((nblk, rows, LANES), F32),
            pltpu.VMEM((nblk, rows, LANES), F32),
        ],
        compiler_params=params(),
        cost_estimate=pl.CostEstimate(flops=2 * 10**9, bytes_accessed=4 * 2**20, transcendentals=0),
        name="science_filter",
    )(info, stamp_rows, stamp_cols, science, edges[:, width:], flags, jnp.asarray(lrow1), jnp.asarray(wcol1))

    first, leftm = place_tables()
    system = pl.pallas_call(
        functools.partial(stamp_kernel, n_tile, nblk),
        out_shape=jax.ShapeDtypeStruct((16, LANES), F32),
        in_specs=[SMEM()] * 3 + [VMEM()] * (nblk + 5),
        out_specs=VMEM(),
        scratch_shapes=[
            pltpu.VMEM((nblk + 2, rows + 2 * HALO, LANES), F32),
            pltpu.VMEM((6, groups * PATCH_ROWS, LANES), F32),
            pltpu.VMEM((NB, depth, LANES), F32),
            pltpu.VMEM((96 * 8, LANES), F32),
        ],
        compiler_params=params(),
        cost_estimate=pl.CostEstimate(flops=10**9, bytes_accessed=2 * 2**20, transcendentals=0),
        name="stamp_sums",
    )(info, stamp_rows, stamp_cols, *blocks, wp, sp, jnp.asarray(stamp_table()), jnp.asarray(first), jnp.asarray(leftm))

    images = pl.pallas_call(
        functools.partial(images_kernel, n_tile, nblk),
        out_shape=jax.ShapeDtypeStruct((nblk, NB, rows, LANES), F32),
        grid=(nblk,),
        in_specs=[SMEM()] + [VMEM()] * (nblk + 2),
        out_specs=pl.BlockSpec((1, NB, rows, LANES), lambda m: (m, 0, 0, 0)),
        scratch_shapes=[
            pltpu.VMEM((nblk + 2, rows + 2 * HALO, LANES), F32),
            pltpu.VMEM((nblk, 6, rows, LANES), BF16),
            pltpu.VMEM((nblk, 6, rows, LANES), BF16),
        ],
        compiler_params=params(),
        cost_estimate=pl.CostEstimate(flops=8 * 10**9, bytes_accessed=16 * 2**20, transcendentals=0),
        name="filtered_images",
    )(info, *blocks, jnp.asarray(lrow6), jnp.asarray(wcol6))

    system = all_sum(system, n_epoch)

    detection, coefficients = pl.pallas_call(
        final_kernel,
        out_shape=(
            jax.ShapeDtypeStruct((rows, cols), F32),
            jax.ShapeDtypeStruct((NB,), F32),
        ),
        grid=(nblk,),
        in_specs=[
            VMEM(),
            pl.BlockSpec((rows, LANES), lambda m: (0, m)),
            pl.BlockSpec((1, NB, rows, LANES), lambda m: (m, 0, 0, 0)),
        ],
        out_specs=(pl.BlockSpec((rows, LANES), lambda m: (0, m)), SMEM()),
        scratch_shapes=[pltpu.VMEM((16, LANES), F32)],
        compiler_params=params(),
        cost_estimate=pl.CostEstimate(flops=10**8, bytes_accessed=16 * 2**20, transcendentals=0),
        name="solve_subtract",
    )(system, d0, images)
    return (detection[None], coefficients)


def solution(mesh):
    return jax.shard_map(
        local,
        mesh=mesh,
        in_specs=(
            P(("patch", "tile"), "epoch"),
            P(("patch", "epoch"), "tile", None),
            P(("patch", "epoch"), "tile", None),
            P(("patch", "epoch"), "tile"),
            P(("patch", "epoch"), "tile"),
        ),
        out_specs=(P(("patch", "epoch"), "tile", None), P("patch")),
        check_vma=False,
    )
```

```python
import functools

import jax
import jax.numpy as jnp
import numpy as np
from jax import lax
from jax.experimental import pallas as pl
from jax.experimental.pallas import tpu as pltpu
from jax.sharding import PartitionSpec as P

STAMP = 32
HALF = 7
TAPS = 15
SIGMAS = (1.0, 2.0, 3.5)
NB = 12
LANES = 128
HALO = 16
WIN = LANES + 2 * HALO
PATCH_ROWS = 48
F32 = jnp.float32
BF16 = jnp.bfloat16
LIMIT = 56 * 1024 * 1024


def split_np(a):
    a = np.asarray(a, np.float32)
    hi = a.astype(BF16)
    lo = (a - hi.astype(np.float32)).astype(BF16)
    return hi, lo


def profiles():
    offsets = np.arange(TAPS, dtype=np.float64) - HALF
    rows = []
    for sigma in SIGMAS:
        gauss = np.exp(-offsets * offsets / (2.0 * sigma * sigma))
        gauss = gauss / gauss.sum()
        rows += [gauss, gauss * offsets / HALF]
    return np.stack(rows)


def psf_profile():
    offsets = np.arange(TAPS, dtype=np.float64) - HALF
    gauss = np.exp(-offsets * offsets / 4.5)
    return gauss / gauss.sum()


def band(profile, size):
    out = np.zeros((size, size))
    for shift in range(TAPS):
        out += profile[shift] * np.eye(size, k=shift - HALF)
    return out


def three_bands(size):
    psf = band(psf_profile(), size)
    return [psf @ band(p, size) for p in profiles()], psf


def pick(matrix, rows, cols):
    cols = np.asarray(cols)
    ok = (cols >= 0) & (cols < matrix.shape[1])
    out = matrix[np.asarray(rows)[:, None], np.clip(cols, 0, matrix.shape[1] - 1)[None, :]]
    return np.where(ok[None, :], out, 0.0)


def starts():
    return (0, LANES, 2 * LANES)


def row_tables():
    size = 3 * LANES
    ops, psf = three_bands(size)

    def stack(ms):
        out = []
        for start in starts():
            rows = np.arange(LANES) + start
            cols = np.arange(WIN) + start - HALO
            hi, lo = split_np(np.concatenate([pick(m, rows, cols) for m in ms], axis=0))
            out.append(np.concatenate([hi, hi, lo], axis=1))
        return np.stack(out)

    return stack(ops), stack([psf])


def column_tables():
    size = 3 * LANES
    ops, psf = three_bands(size)

    def one(matrix, start):
        lane = np.arange(LANES)
        cols = np.concatenate([start + lane, np.where(lane < 64, start + LANES + lane, start - LANES + lane)])
        return pick(matrix, np.arange(LANES) + start, cols).T

    model = []
    for start in starts():
        per = []
        for s in range(3):
            both = np.concatenate([one(ops[2 * s], start), one(ops[2 * s + 1], start)], axis=1)
            per.append(np.stack(split_np(both)))
        model.append(np.stack(per))
    return np.stack(model), np.stack([np.stack(split_np(one(psf, start))) for start in starts()])


def stamp_table():
    prof = profiles()
    out = np.zeros((256, 6, LANES))
    for q in range(4):
        for c in range(STAMP):
            for v in range(TAPS):
                out[q * 64 + c + v, :, q * STAMP + c] = prof[:, v]
    return np.stack(split_np(out.reshape(256, 6 * LANES)))


def pair_list():
    return [(k, l) for k in range(NB) for l in range(k, NB)] + [(k, NB) for k in range(NB)]


def place_tables():
    pairs = pair_list()
    first = np.zeros((2, 96, LANES), np.float32)
    left = np.zeros((16, 192), np.float32)
    for p, (k, l) in enumerate(pairs):
        first[0, p, l] = 1.0
        left[k, p] = 1.0
        if l < NB and l != k:
            first[1, p, k] = 1.0
            left[l, 96 + p] = 1.0
    return first, left


def dot(a, b):
    return jnp.dot(a, b, preferred_element_type=F32)


def split(x):
    hi = x.astype(BF16)
    lo = (x - hi.astype(F32)).astype(BF16)
    return hi, lo


def stack3(x):
    hi, lo = split(x)
    return jnp.concatenate([hi, lo, hi], axis=0)


def params(**kw):
    return pltpu.CompilerParams(vmem_limit_bytes=LIMIT, **kw)


VMEM = functools.partial(pl.BlockSpec, memory_space=pltpu.VMEM)
SMEM = functools.partial(pl.BlockSpec, memory_space=pltpu.SMEM)


def lane_index(shape):
    return lax.broadcasted_iota(jnp.int32, shape, len(shape) - 1)


def variant(tile, b, n_tile, nrow):
    v = jnp.int32(1)
    if b == 0:
        v = jnp.where(tile == 0, 0, v)
    if b == nrow - 1:
        v = jnp.where(tile == n_tile - 1, 2, v)
    return v


def window_rows(tile, b, n_tile, nrow, own, edge):
    size = nrow * LANES
    low, high = b * LANES - HALO, (b + 1) * LANES + HALO
    parts = []
    if low < 0:
        parts.append(jnp.where(tile == 0, 0.0, edge()))
    parts.append(own(max(low, 0), min(high, size)))
    if high > size:
        parts.append(jnp.where(tile == n_tile - 1, 0.0, edge()))
    return jnp.concatenate(parts, axis=0)


def science_kernel(n_tile, info, sci, edge, lrow, wcol, after, *refs):
    count = len(refs) // 2 - 1
    d0, mid, sems = refs[count], refs[-2], refs[-1]
    copies = [pltpu.make_async_copy(refs[i], refs[count + 1 + i], sems.at[i]) for i in range(count)]
    for copy in copies:
        copy.start()
    tile = info[0]
    nblk, rows = sci.shape[:2]
    nrow = rows // LANES
    for b in range(nrow):
        left = lrow[variant(tile, b, n_tile, nrow)]
        for m in range(0, nblk, 2):

            def own(lo, hi):
                return jnp.concatenate([sci[m, lo:hi, :], sci[m + 1, lo:hi, :]], axis=1)

            x = window_rows(tile, b, n_tile, nrow, own, lambda: edge[:, m * LANES : (m + 2) * LANES])
            y = dot(left, stack3(x))
            mid[m, b * LANES : (b + 1) * LANES, :] = y[:, :LANES]
            mid[m + 1, b * LANES : (b + 1) * LANES, :] = y[:, LANES:]
    lane = lane_index((rows, LANES))
    for m in range(nblk):
        v = 0 if m == 0 else (2 if m == nblk - 1 else 1)
        rim = jnp.where(lane < 64, mid[min(m + 1, nblk - 1)], mid[max(m - 1, 0)])
        hi, lo = split(jnp.concatenate([mid[m], rim], axis=1))
        d0[:, m * LANES : (m + 1) * LANES] = dot(hi, wcol[v, 0]) + dot(lo, wcol[v, 0]) + dot(hi, wcol[v, 1])
    for copy in copies:
        copy.wait()


def load_kernel(n_tile, stamps, info, *refs):
    sci, flags, lrow, *tables = refs[: len(refs) // 2 - 2]
    wp, sp, sb, lout, *outs = refs[len(refs) // 2 - 2 : -3]
    fb, sems, more = refs[-3:]
    tile = info[0]
    nblk, rows = sb.shape[:2]
    nrow = rows // LANES
    early = []
    for m in range(nblk):
        piece = slice(m * LANES, (m + 1) * LANES)
        early.append(pltpu.make_async_copy(sci.at[:, piece], sb.at[m], sems.at[m]))
        early.append(pltpu.make_async_copy(flags.at[:, piece], fb.at[m], sems.at[nblk + m]))
    late = [
        pltpu.make_async_copy(lrow.at[variant(tile, b, n_tile, nrow)], lout.at[b], more.at[b]) for b in range(nrow)
    ]
    late += [pltpu.make_async_copy(t, o, more.at[nrow + i]) for i, (t, o) in enumerate(zip(tables, outs))]
    for copy in early + late:
        copy.start()
    for copy in early:
        copy.wait()
    lane = lane_index((STAMP, LANES))
    for g in range(stamps // 4):
        w = jnp.zeros((STAMP, LANES), F32)
        s = jnp.zeros((STAMP, LANES), F32)
        for q in range(4):
            top = info[1 + g * 4 + q]
            left = info[1 + stamps + g * 4 + q]
            blk = left // LANES
            off = left - blk * LANES
            nxt = jnp.minimum(blk + 1, nblk - 1)
            shift = lax.rem(q * STAMP - off + LANES, LANES)
            near = lane < q * STAMP - off + LANES
            here = (lane >= q * STAMP) & (lane < (q + 1) * STAMP)

            def window(ref):
                a = pltpu.roll(ref[blk, pl.ds(top, STAMP), :], shift, 1)
                b = pltpu.roll(ref[nxt, pl.ds(top, STAMP), :], shift, 1)
                return jnp.where(near, a, b)

            w = jnp.where(here & (window(fb) == 0), 1.0, w)
            s = jnp.where(here, window(sb), s)
        wp[g * STAMP : (g + 1) * STAMP, :] = w
        sp[g * STAMP : (g + 1) * STAMP, :] = jnp.where(w > 0.0, s, 0.0)
    for copy in late:
        copy.wait()


def assemble(info, first, n_tile, blocks, t):
    tile = info[0]
    rows = blocks[0].shape[0] - HALO
    for m in (0, len(blocks) + 1):
        t[m] = jnp.zeros(t.shape[1:], F32)
    for slot, block in enumerate(blocks):
        at = info[first + slot] + 1
        e = block[rows:, :]
        t[at, 0:HALO, :] = jnp.where(tile == 0, 0.0, e)
        t[at, HALO : HALO + rows, :] = block[0:rows, :]
        t[at, HALO + rows :, :] = jnp.where(tile == n_tile - 1, 0.0, e)


def stamp_kernel(n_tile, nblk, stamps, info, *refs):
    blocks = refs[:nblk]
    wp, sp, mcol, first, leftm, system, t, y, images, sums = refs[nblk:]
    assemble(info, 1 + 2 * stamps, n_tile, blocks, t)
    groups = stamps // 4
    lane = lane_index((PATCH_ROWS, LANES))
    prof = profiles()
    xs = []
    for g in range(groups):
        halves = []
        for pair in range(2):
            parts = []
            for h in range(2):
                j = g * 4 + pair * 2 + h
                start = info[1 + stamps + j] + (LANES - HALF)
                blk = start // LANES
                off = start - blk * LANES
                shift = lax.rem(64 * h - off + LANES, LANES)
                rows = pl.ds(info[1 + j] + (HALO - HALF), PATCH_ROWS)
                a = pltpu.roll(t[blk, rows, :], shift, 1)
                b = pltpu.roll(t[blk + 1, rows, :], shift, 1)
                parts.append(jnp.where(lane < 64 * h - off + LANES, a, b))
            halves.append(jnp.where(lane < 64, parts[0], parts[1]))
        xs.append(jnp.concatenate(halves, axis=1))
    hi, lo = split(jnp.concatenate(xs, axis=0))
    for p in range(6):
        piece = slice(p * LANES, (p + 1) * LANES)
        wh = mcol[0, :, piece]
        y[p] = dot(hi, wh) + dot(lo, wh) + dot(hi, mcol[1, :, piece])
    for s in range(3):
        gauss = prof[2 * s]
        for j in range(2):
            for g in range(groups):
                base = g * PATCH_ROWS

                def at(o):
                    return y[2 * s + j, base + HALF + o : base + HALF + o + STAMP, :]

                even = at(0) * np.float32(gauss[HALF])
                odd = None
                for d in range(1, HALF + 1):
                    up, down = at(d), at(-d)
                    even = even + (up + down) * np.float32(gauss[HALF + d])
                    term = (up - down) * np.float32(gauss[HALF + d] * d / HALF)
                    odd = term if odd is None else odd + term
                images[4 * s + 2 * j, g * STAMP : (g + 1) * STAMP, :] = even
                images[4 * s + 2 * j + 1, g * STAMP : (g + 1) * STAMP, :] = odd
    depth = groups * STAMP
    w = wp[...]
    weighted = None
    for p, (k, l) in enumerate(pair_list()):
        if l == NB:
            prod = sp[...] * images[k]
        else:
            if l == k:
                weighted = w * images[k]
            prod = weighted * images[l]
        sums[p * 8 : (p + 1) * 8, :] = jnp.sum(prod.reshape(depth // 8, 8, LANES), axis=0)
    used = len(pair_list())
    sums[used * 8 :, :] = jnp.zeros((96 * 8 - used * 8, LANES), F32)
    total = sums[pl.ds(0, 96, stride=8), :]
    for r in range(1, 8):
        total = total + sums[pl.ds(r, 96, stride=8), :]
    total = jnp.sum(total, axis=1, keepdims=True)
    spread = jnp.concatenate([total * first[0], total * first[1]], axis=0)
    system[...] = jnp.dot(leftm[...], spread, preferred_element_type=F32, precision=lax.Precision.HIGHEST)


def rows_kernel(n_tile, first, slots, info, lrow, after, *refs):
    blocks = refs[: len(slots)]
    rhi, rlo = refs[-2:]
    tile = info[0]
    rows = rhi.shape[2]
    nrow = rows // LANES
    for b in range(nrow):
        left = lrow[b]
        xs = [
            window_rows(tile, b, n_tile, nrow, lambda lo, hi: block[lo:hi, :], lambda: block[rows:, :])
            for block in blocks
        ]
        hi, lo = split(dot(left, stack3(jnp.concatenate(xs, axis=1) if len(xs) > 1 else xs[0])))
        for h, slot in enumerate(slots):
            at = info[first + slot]
            for p in range(6):
                piece = (slice(p * LANES, (p + 1) * LANES), slice(h * LANES, (h + 1) * LANES))
                rhi[at, p, b * LANES : (b + 1) * LANES, :] = hi[piece]
                rlo[at, p, b * LANES : (b + 1) * LANES, :] = lo[piece]


def columns_kernel(nblk, first, places, info, rhi, rlo, wcol, *refs):
    out = refs[-1]
    rows = rhi.shape[2]
    lane = lane_index((2 * rows, LANES))
    for place in places:
        m = info[first + place]
        v = jnp.where(m == 0, 0, jnp.where(m == nblk - 1, 2, 1))
        after = jnp.minimum(m + 1, nblk - 1)
        before = jnp.maximum(m - 1, 0)
        for s in range(3):

            def window(ref):
                def get(i):
                    return ref[i, 2 * s : 2 * s + 2].reshape(2 * rows, LANES)

                rim = jnp.where(lane < 64, get(after), get(before))
                return jnp.concatenate([get(m), rim], axis=1)

            hi, lo = window(rhi), window(rlo)
            q = dot(hi, wcol[v, s, 0]) + dot(lo, wcol[v, s, 0]) + dot(hi, wcol[v, s, 1])
            for i in range(2):
                for j in range(2):
                    out[m, 4 * s + i + 2 * j] = q[i * rows : (i + 1) * rows, j * LANES : (j + 1) * LANES]


def final_kernel(step, system, d0, images, detection, coefficients, solved):
    @pl.when(pl.program_id(0) == 0)
    def _():
        a = system[...]
        row = lax.broadcasted_iota(jnp.int32, a.shape, 0)
        lane = lane_index(a.shape)
        diag = (row == lane) & (row < NB)
        trace = jnp.sum(jnp.sum(jnp.where(diag, a, 0.0), axis=1, keepdims=True), axis=0, keepdims=True)
        a = a + jnp.where(diag, 0.05 * trace / NB, 0.0)
        for k in range(NB):
            pivot = a[k : k + 1, :] / a[k : k + 1, k : k + 1]
            a = jnp.where(row == k, pivot, a - a[:, k : k + 1] * pivot)
        solved[...] = jnp.broadcast_to(a[:, NB : NB + 1], a.shape)
        for k in range(NB):
            coefficients[k] = solved[k, 0]

    for h in range(step):
        m = pl.program_id(0) * step + h
        total = d0[:, h * LANES : (h + 1) * LANES]
        for k in range(NB):
            total = total - solved[k : k + 1, :] * images[m, k]
        detection[:, h * LANES : (h + 1) * LANES] = total


def ring_order(count):
    return list(range(0, count, 2)) + list(range(count - 1, 0, -2))


def swap(x):
    return lax.ppermute(x, "tile", [(0, 1), (1, 0)])


def gather_ring(block, count):
    ring = ring_order(count)
    ahead = [(ring[i], ring[(i + 1) % count]) for i in range(count)]
    back = [(t, s) for s, t in ahead]
    out = [block]
    fwd = bwd = block
    for step in range(count // 2):
        fwd = lax.ppermute(fwd, "epoch", ahead)
        out.append(fwd)
        if step < count // 2 - 1:
            bwd = lax.ppermute(bwd, "epoch", back)
            out.append(bwd)
    return out


def ring_table(count):
    ring = ring_order(count)
    table = np.zeros((count, count), np.int32)
    for i, me in enumerate(ring):
        order = [me]
        for step in range(1, count // 2 + 1):
            order.append(ring[(i - step) % count])
            if step < count // 2:
                order.append(ring[(i + step) % count])
        table[me] = order
    return table


def all_sum(x, count, beside):
    beside[0](x)
    x = x + swap(x)
    if count & (count - 1):
        for f in beside[1:]:
            f(x)
        return lax.psum(x, "epoch")
    steps = count.bit_length() - 1
    for i in range(steps):
        for f in beside[1 + i :: steps]:
            f(x)
        x = x + lax.ppermute(x, "epoch", [(j, j ^ (1 << i)) for j in range(count)])
    return x


def place_table(last, nblk):
    return np.stack([(x + 2 + np.arange(nblk)) % nblk for x in last]).astype(np.int32)


def in_vmem(x):
    return pltpu.with_memory_space_constraint(x, pltpu.VMEM)


ANY = functools.partial(pl.BlockSpec, memory_space=pl.ANY)
HBM = functools.partial(pl.BlockSpec, memory_space=pltpu.HBM)


def call(kernel, name, out, ins, limit, flops, scratch=(), aliases=None, outside=(), hbm=()):
    ins = [pltpu.with_memory_space_constraint(x, pltpu.HBM) if i in hbm else x for i, x in enumerate(ins)]

    def spec(i, x):
        if i in outside:
            return ANY()
        if i in hbm:
            return HBM()
        return SMEM() if x.ndim == 1 else VMEM()

    return pl.pallas_call(
        kernel,
        out_shape=out,
        in_specs=[spec(i, x) for i, x in enumerate(ins)],
        out_specs=jax.tree.map(lambda _: VMEM(), out, is_leaf=lambda x: hasattr(x, "shape")),
        scratch_shapes=scratch,
        input_output_aliases=aliases or {},
        compiler_params=pltpu.CompilerParams(vmem_limit_bytes=limit * 2**20),
        cost_estimate=pl.CostEstimate(flops=flops, bytes_accessed=2**20, transcendentals=0),
        name=name,
    )(*ins)


def local(template, science, flags, stamp_rows, stamp_cols):
    n_tile = lax.axis_size("tile")
    n_epoch = lax.axis_size("epoch")
    rows, width = template.shape
    science, flags = science[0], flags[0]
    cols = science.shape[1]
    nblk = cols // LANES
    nrow = rows // LANES
    stamps = stamp_rows.shape[1]
    groups = stamps // 4
    depth = groups * STAMP
    tile = lax.axis_index("tile")

    def edge_of(x):
        return jnp.where(tile == 0, x[-HALO:], x[:HALO])

    tall = jnp.concatenate([template, swap(edge_of(template))], axis=0)
    _, later, stamp_rows, stamp_cols = lax.optimization_barrier((tall, science, stamp_rows, stamp_cols))
    science_edge = swap(edge_of(later))
    if width == LANES:
        blocks = gather_ring(tall, n_epoch)
        table = np.concatenate([ring_table(n_epoch), place_table(ring_table(n_epoch)[:, -1], nblk)], axis=1)
        order = jnp.asarray(table)[lax.axis_index("epoch")]
    else:
        whole = lax.all_gather(tall, "epoch", axis=1, tiled=True)
        blocks = [whole[:, m * LANES : (m + 1) * LANES] for m in range(nblk)]
        order = jnp.asarray(np.concatenate([np.arange(nblk), place_table(np.full(1, nblk - 1), nblk)[0]]).astype(np.int32))
    info = jnp.concatenate([tile[None].astype(jnp.int32), stamp_rows[0], stamp_cols[0], order])
    at_slots = 1 + 2 * stamps
    at_places = at_slots + nblk

    lrow6, lrow1 = row_tables()
    wcol6, wcol1 = column_tables()
    first, leftm = place_tables()
    lrow6 = jnp.asarray(lrow6)
    tables = [jnp.asarray(x) for x in (lrow1, wcol1)]
    later_tables = [jnp.asarray(x) for x in (stamp_table(), wcol6, first, leftm)]

    def like(xs):
        return tuple(pltpu.VMEM(x.shape, x.dtype) for x in xs)

    wp, sp, sci, lrow6, lrow1, wcol1 = map(in_vmem, call(
        functools.partial(load_kernel, n_tile, stamps),
        "load_and_cut",
        (
            pltpu.VMEM((depth, LANES), F32),
            pltpu.VMEM((depth, LANES), F32),
            pltpu.VMEM((nblk, rows, LANES), F32),
            pltpu.VMEM((nrow,) + lrow6.shape[1:], BF16),
        )
        + like(tables),
        [info, science, flags, lrow6] + tables,
        8,
        2 * 10**9,
        [
            pltpu.VMEM((nblk, rows, LANES), jnp.int32),
            pltpu.SemaphoreType.DMA((2 * nblk,)),
            pltpu.SemaphoreType.DMA((nrow + len(tables),)),
        ],
        hbm=range(1, 4 + len(tables)),
    ))
    d0, mcol, wcol6, first, leftm = map(in_vmem, call(
        functools.partial(science_kernel, n_tile),
        "science_filter",
        (pltpu.VMEM((rows, cols), F32),) + like(later_tables),
        [info, sci, science_edge, lrow1, wcol1, blocks[1]] + later_tables,
        12,
        2 * 10**9,
        [pltpu.VMEM((nblk, rows, LANES), F32), pltpu.SemaphoreType.DMA((len(later_tables),))],
        outside=(5,),
        hbm=range(6, 6 + len(later_tables)),
    ))

    def row_filters(slots, r):
        ins = [info, lrow6, blocks[1] if slots[0] < nblk - 1 else d0] + [blocks[slot] for slot in slots] + [in_vmem(x) for x in r]
        n = len(ins)
        return call(
            functools.partial(rows_kernel, n_tile, at_slots, slots),
            "template_rows",
            (pltpu.VMEM((nblk, 6, rows, LANES), BF16),) * 2,
            ins,
            12,
            10**9,
            aliases={n - 2: 0, n - 1: 1} if r else None,
            outside=(2,),
        )

    def column_filters(places, r, q, after):
        ins = [info] + [in_vmem(x) for x in r] + [wcol6, after] + [in_vmem(x) for x in q]
        return call(
            functools.partial(columns_kernel, nblk, at_places, places),
            "template_columns",
            pltpu.VMEM((nblk, NB, rows, LANES), F32),
            ins,
            12,
            10**9 * len(places),
            aliases={5: 0} if q else None,
            outside=(4,),
        )

    r = ()
    for slots in [(0,)] + [(i, i + 1) for i in range(1, nblk - 1, 2)]:
        r = row_filters(slots, r)
    state = dict(r=r, q=())

    def more_columns(places):
        def go(x):
            state["q"] = (column_filters(places, state["r"], state["q"], x),)

        return go

    def last_rows(x):
        state["r"] = row_filters((nblk - 1,), state["r"])

    groups_of = [tuple(range(i, i + 2)) for i in range(0, nblk, 2)]
    more_columns(groups_of[0])(blocks[-2])

    system = call(
        functools.partial(stamp_kernel, n_tile, nblk, stamps),
        "stamp_sums",
        pltpu.VMEM((16, LANES), F32),
        [info, *blocks, wp, sp, mcol, first, leftm],
        12,
        10**9,
        [
            pltpu.VMEM((nblk + 2, rows + 2 * HALO, LANES), F32),
            pltpu.VMEM((6, groups * PATCH_ROWS, LANES), F32),
            pltpu.VMEM((NB, depth, LANES), F32),
            pltpu.VMEM((96 * 8, LANES), F32),
        ],
    )
    system = all_sum(system, n_epoch, [last_rows] + [more_columns(g) for g in groups_of[1:]])

    step = 2
    detection, coefficients = pl.pallas_call(
        functools.partial(final_kernel, step),
        out_shape=(
            jax.ShapeDtypeStruct((rows, cols), F32),
            jax.ShapeDtypeStruct((NB,), F32),
        ),
        grid=(nblk // step,),
        in_specs=[
            VMEM(),
            pl.BlockSpec((rows, step * LANES), lambda m: (0, m)),
            VMEM(),
        ],
        out_specs=(pl.BlockSpec((rows, step * LANES), lambda m: (0, m)), SMEM()),
        scratch_shapes=[pltpu.VMEM((16, LANES), F32)],
        compiler_params=pltpu.CompilerParams(vmem_limit_bytes=8 * 2**20),
        cost_estimate=pl.CostEstimate(flops=10**8, bytes_accessed=16 * 2**20, transcendentals=0),
        name="solve_subtract",
    )(system, d0, in_vmem(state["q"][0]))
    return (detection[None], coefficients)


def solution(mesh):
    return jax.shard_map(
        local,
        mesh=mesh,
        in_specs=(
            P(("patch", "tile"), "epoch"),
            P(("patch", "epoch"), "tile", None),
            P(("patch", "epoch"), "tile", None),
            P(("patch", "epoch"), "tile"),
            P(("patch", "epoch"), "tile"),
        ),
        out_specs=(P(("patch", "epoch"), "tile", None), P("patch")),
        check_vma=False,
    )
```

```python
import functools

import jax
import jax.numpy as jnp
import numpy as np
from jax import lax
from jax.experimental import pallas as pl
from jax.experimental.pallas import tpu as pltpu
from jax.sharding import PartitionSpec as P

STAMP = 32
HALF = 7
TAPS = 15
SIGMAS = (1.0, 2.0, 3.5)
NB = 12
LANES = 128
HALO = 16
WIN = LANES + 2 * HALO
PATCH_ROWS = 48
F32 = jnp.float32
BF16 = jnp.bfloat16
LIMIT = 56 * 1024 * 1024


def split_np(a):
    a = np.asarray(a, np.float32)
    hi = a.astype(BF16)
    lo = (a - hi.astype(np.float32)).astype(BF16)
    return hi, lo


def profiles():
    offsets = np.arange(TAPS, dtype=np.float64) - HALF
    rows = []
    for sigma in SIGMAS:
        gauss = np.exp(-offsets * offsets / (2.0 * sigma * sigma))
        gauss = gauss / gauss.sum()
        rows += [gauss, gauss * offsets / HALF]
    return np.stack(rows)


def psf_profile():
    offsets = np.arange(TAPS, dtype=np.float64) - HALF
    gauss = np.exp(-offsets * offsets / 4.5)
    return gauss / gauss.sum()


def band(profile, size):
    out = np.zeros((size, size))
    for shift in range(TAPS):
        out += profile[shift] * np.eye(size, k=shift - HALF)
    return out


def three_bands(size):
    psf = band(psf_profile(), size)
    return [psf @ band(p, size) for p in profiles()], psf


def pick(matrix, rows, cols):
    cols = np.asarray(cols)
    ok = (cols >= 0) & (cols < matrix.shape[1])
    out = matrix[np.asarray(rows)[:, None], np.clip(cols, 0, matrix.shape[1] - 1)[None, :]]
    return np.where(ok[None, :], out, 0.0)


def starts():
    return (0, LANES, 2 * LANES)


def row_tables():
    size = 3 * LANES
    ops, psf = three_bands(size)

    def stack(ms):
        out = []
        for start in starts():
            rows = np.arange(LANES) + start
            cols = np.arange(WIN) + start - HALO
            hi, lo = split_np(np.concatenate([pick(m, rows, cols) for m in ms], axis=0))
            out.append(np.concatenate([hi, hi, lo], axis=1))
        return np.stack(out)

    return stack(ops), stack([psf])


def column_tables():
    size = 3 * LANES
    ops, psf = three_bands(size)
    lane = np.arange(LANES)

    def own(matrix, start):
        return split_np(pick(matrix, lane + start, lane + start).T)

    def rim(matrix, start):
        side = np.where(lane < 64, start + LANES + lane, start - LANES + lane)
        return split_np(pick(matrix, lane + start, side).T)

    def model(matrix, start):
        hi, lo = own(matrix, start)
        rhi, rlo = rim(matrix, start)
        packed = np.zeros_like(rhi)
        for at in list(range(2 * HALF)) + list(range(LANES - 2 * HALF, LANES)):
            packed[at] = rhi[at]
            packed[(at + 64) % LANES] = rlo[at]
            packed[(at + 96) % LANES] = rhi[at]
        return np.stack([np.concatenate([hi, hi]), np.concatenate([lo, packed])])

    def science(start):
        return np.stack([np.concatenate(p) for p in zip(own(psf, start), rim(psf, start))])

    models = [
        [np.concatenate([model(ops[2 * s], start), model(ops[2 * s + 1], start)], axis=2) for s in range(3)]
        for start in starts()
    ]
    return np.array(models), np.stack([science(start) for start in starts()])


def stamp_table():
    prof = profiles()
    out = np.zeros((256, 6, LANES))
    for q in range(4):
        for c in range(STAMP):
            for v in range(TAPS):
                out[q * 64 + c + v, :, q * STAMP + c] = prof[:, v]
    return np.stack(split_np(out.reshape(256, 6 * LANES)))


def dot(a, b):
    return jnp.dot(a, b, preferred_element_type=F32)


def split(x):
    hi = x.astype(BF16)
    lo = (x - hi.astype(F32)).astype(BF16)
    return hi, lo


def stack3(x):
    hi, lo = split(x)
    return jnp.concatenate([hi, lo, hi], axis=0)


def params(**kw):
    return pltpu.CompilerParams(vmem_limit_bytes=LIMIT, **kw)


VMEM = functools.partial(pl.BlockSpec, memory_space=pltpu.VMEM)
SMEM = functools.partial(pl.BlockSpec, memory_space=pltpu.SMEM)


def row_index(shape):
    return lax.broadcasted_iota(jnp.int32, shape, len(shape) - 2)


def lane_index(shape):
    return lax.broadcasted_iota(jnp.int32, shape, len(shape) - 1)


def ring_place(step, count):
    me = lax.axis_index("epoch")
    at = jnp.where(lax.rem(me, 2) == 0, me // 2, count - 1 - me // 2)
    at = lax.rem(at + step + count, count)
    return jnp.where(at < count // 2, 2 * at, 2 * (count - 1 - at) + 1)


def slot_block(slot, nblk, ring):
    if not ring:
        return jnp.int32(slot)
    step = (slot + 1) // 2
    return ring_place(step if slot % 2 == 0 else -step, nblk)


def place_block(place, nblk, ring):
    return lax.rem(slot_block(nblk - 1, nblk, ring) + 2 + place, nblk)


def variant(tile, b, n_tile, nrow):
    v = jnp.int32(1)
    if b == 0:
        v = jnp.where(tile == 0, 0, v)
    if b == nrow - 1:
        v = jnp.where(tile == n_tile - 1, 2, v)
    return v


def window_rows(tile, b, n_tile, nrow, own, edge):
    size = nrow * LANES
    low, high = b * LANES - HALO, (b + 1) * LANES + HALO
    parts = []
    if low < 0:
        parts.append(jnp.where(tile == 0, 0.0, edge()))
    parts.append(own(max(low, 0), min(high, size)))
    if high > size:
        parts.append(jnp.where(tile == n_tile - 1, 0.0, edge()))
    return jnp.concatenate(parts, axis=0)


def science_kernel(n_tile, sci, edge, lrow, wcol, after, *refs):
    count = len(refs) // 2 - 1
    d0, mid, sems = refs[count], refs[-2], refs[-1]
    copies = [pltpu.make_async_copy(refs[i], refs[count + 1 + i], sems.at[i]) for i in range(count)]
    for copy in copies:
        copy.start()
    tile = lax.axis_index("tile")
    nblk, rows = sci.shape[:2]
    nrow = rows // LANES
    for b in range(nrow):
        left = lrow[variant(tile, b, n_tile, nrow)]
        for m in range(0, nblk, 2):

            def own(lo, hi):
                return jnp.concatenate([sci[m, lo:hi, :], sci[m + 1, lo:hi, :]], axis=1)

            x = window_rows(tile, b, n_tile, nrow, own, lambda: edge[:, m * LANES : (m + 2) * LANES])
            y = dot(left, stack3(x))
            mid[m, b * LANES : (b + 1) * LANES, :] = y[:, :LANES]
            mid[m + 1, b * LANES : (b + 1) * LANES, :] = y[:, LANES:]
    lane = lane_index((rows, LANES))
    for m in range(nblk):
        v = 0 if m == 0 else (2 if m == nblk - 1 else 1)
        rim = jnp.where(lane < 64, mid[min(m + 1, nblk - 1)], mid[max(m - 1, 0)])
        hi, lo = split(jnp.concatenate([mid[m], rim], axis=1))
        d0[:, m * LANES : (m + 1) * LANES] = dot(hi, wcol[v, 0]) + dot(lo, wcol[v, 0]) + dot(hi, wcol[v, 1])
    for copy in copies:
        copy.wait()


def load_kernel(n_tile, *refs):
    half = len(refs) // 2
    after, sci, flags, lrow, *tables = refs[:half]
    sb, fb, lout, *outs = refs[half:-1]
    sems = refs[-1]
    tile = lax.axis_index("tile")
    nblk, rows = sb.shape[:2]
    nrow = rows // LANES
    pairs = []
    for m in range(nblk):
        piece = slice(m * LANES, (m + 1) * LANES)
        pairs += [(sci.at[:, piece], sb.at[m]), (flags.at[:, piece], fb.at[m])]
    pairs += [(lrow.at[variant(tile, b, n_tile, nrow)], lout.at[b]) for b in range(nrow)]
    pairs += list(zip(tables, outs))
    copies = [pltpu.make_async_copy(a, b, sems.at[i]) for i, (a, b) in enumerate(pairs)]
    for copy in copies:
        copy.start()
    for copy in copies:
        copy.wait()


def cut_kernel(info, sb, fb, after, wp, sp):
    stamps = info.shape[0] // 2
    nblk = sb.shape[0]
    lane = lane_index((STAMP, LANES))
    for g in range(stamps // 4):
        w = jnp.zeros((STAMP, LANES), F32)
        s = jnp.zeros((STAMP, LANES), F32)
        for q in range(4):
            top = info[g * 4 + q]
            left = info[stamps + g * 4 + q]
            blk = left // LANES
            off = left - blk * LANES
            nxt = jnp.minimum(blk + 1, nblk - 1)
            shift = lax.rem(q * STAMP - off + LANES, LANES)
            near = lane < q * STAMP - off + LANES
            here = (lane >= q * STAMP) & (lane < (q + 1) * STAMP)

            def window(ref):
                a = pltpu.roll(ref[blk, pl.ds(top, STAMP), :], shift, 1)
                b = pltpu.roll(ref[nxt, pl.ds(top, STAMP), :], shift, 1)
                return jnp.where(near, a, b)

            w = jnp.where(here & (window(fb) == 0), 1.0, w)
            s = jnp.where(here, window(sb), s)
        wp[g * STAMP : (g + 1) * STAMP, :] = w
        sp[g * STAMP : (g + 1) * STAMP, :] = jnp.where(w > 0.0, s, 0.0)


def put_block(n_tile, block, at, t):
    tile = lax.axis_index("tile")
    rows = block.shape[0] - HALO
    e = block[rows:, :]
    t[at + 1, 0:HALO, :] = jnp.where(tile == 0, 0.0, e)
    t[at + 1, HALO : HALO + rows, :] = block[0:rows, :]
    t[at + 1, HALO + rows :, :] = jnp.where(tile == n_tile - 1, 0.0, e)


def stamp_kernel(n_tile, nblk, ring, info, last, t_in, wp, sp, mcol, after, system, t, y, images):
    stamps = info.shape[0] // 2
    put_block(n_tile, last, slot_block(nblk - 1, nblk, ring), t)
    groups = stamps // 4
    lane = lane_index((PATCH_ROWS, LANES))
    prof = profiles()
    xs = []
    for g in range(groups):
        halves = []
        for pair in range(2):
            parts = []
            for h in range(2):
                j = g * 4 + pair * 2 + h
                start = info[stamps + j] + (LANES - HALF)
                blk = start // LANES
                off = start - blk * LANES
                shift = lax.rem(64 * h - off + LANES, LANES)
                rows = pl.ds(info[j] + (HALO - HALF), PATCH_ROWS)
                a = pltpu.roll(t[blk, rows, :], shift, 1)
                b = pltpu.roll(t[blk + 1, rows, :], shift, 1)
                parts.append(jnp.where(lane < 64 * h - off + LANES, a, b))
            halves.append(jnp.where(lane < 64, parts[0], parts[1]))
        xs.append(jnp.concatenate(halves, axis=1))
    hi, lo = split(jnp.concatenate(xs, axis=0))
    both = jnp.concatenate([hi, lo], axis=0)
    depth = groups * PATCH_ROWS
    for p in range(0, 6, 2):
        piece = slice(p * LANES, (p + 2) * LANES)
        main = dot(both, mcol[0, :, piece])
        total = main[:depth] + main[depth:] + dot(hi, mcol[1, :, piece])
        y[p] = total[:, :LANES]
        y[p + 1] = total[:, LANES:]
    for s in range(3):
        gauss = prof[2 * s]
        for j in range(2):
            for g in range(groups):
                base = g * PATCH_ROWS

                def at(o):
                    return y[2 * s + j, base + HALF + o : base + HALF + o + STAMP, :]

                even = at(0) * np.float32(gauss[HALF])
                odd = None
                for d in range(1, HALF + 1):
                    up, down = at(d), at(-d)
                    even = even + (up + down) * np.float32(gauss[HALF + d])
                    term = (up - down) * np.float32(gauss[HALF + d] * d / HALF)
                    odd = term if odd is None else odd + term
                images[4 * s + 2 * j, g * STAMP : (g + 1) * STAMP, :] = even
                images[4 * s + 2 * j + 1, g * STAMP : (g + 1) * STAMP, :] = odd
    depth = groups * STAMP
    row = row_index((8, LANES))
    lane = lane_index((8, LANES))
    zero = jnp.zeros((8, LANES), F32)
    tiles = [[zero, zero] for _ in range(NB + 1)]

    def collect(k, l, x):
        tiles[l][k // 8] = jnp.where(row == k % 8, x, tiles[l][k // 8])

    w = wp[...]
    for k in range(NB):
        weighted = w * images[k]
        for l in range(k, NB + 1):
            prod = weighted * images[l] if l < NB else sp[...] * images[k]
            x = jnp.sum(prod.reshape(depth // 8, 8, LANES), axis=0)
            for d in (4, 2, 1):
                x = x + pltpu.roll(x, d, 0)
            collect(k, l, x)
            if k < l < NB:
                collect(l, k, x)
    for h in range(2):
        out = zero
        for l in range(NB + 1):
            out = jnp.where(lane == l, jnp.sum(tiles[l][h], axis=1, keepdims=True), out)
        system[h * 8 : (h + 1) * 8, :] = out


def rows_kernel(n_tile, slots, ring, store, lrow, after, *refs):
    blocks = refs[: len(slots)]
    rhi, rlo = refs[-3:-1] if store else refs[-2:]
    tile = lax.axis_index("tile")
    nblk, _, rows = rhi.shape[:3]
    nrow = rows // LANES
    places = [slot_block(slot, nblk, ring) for slot in slots]
    if store:
        t = refs[-1]
        if slots[0] == 0:
            t[0] = jnp.zeros(t.shape[1:], F32)
            t[nblk + 1] = jnp.zeros(t.shape[1:], F32)
        for block, at in zip(blocks, places):
            put_block(n_tile, block, at, t)
    for b in range(nrow):
        xs = [
            window_rows(tile, b, n_tile, nrow, lambda lo, hi: block[lo:hi, :], lambda: block[rows:, :])
            for block in blocks
        ]
        hi, lo = split(dot(lrow[b], stack3(jnp.concatenate(xs, axis=1) if len(xs) > 1 else xs[0])))
        for h, at in enumerate(places):
            for p in range(6):
                piece = (slice(p * LANES, (p + 1) * LANES), slice(h * LANES, (h + 1) * LANES))
                rhi[at, p, b * LANES : (b + 1) * LANES, :] = hi[piece]
                rlo[at, p, b * LANES : (b + 1) * LANES, :] = lo[piece]


def columns_kernel(nblk, places, ring, rhi, rlo, wcol, after, *refs):
    out = refs[-1]
    rows = rhi.shape[2]
    lane = lane_index((2 * rows, LANES))
    reach = 2 * HALF
    in_low = (lane >= 96 - reach) & (lane < 96 + reach)
    in_high = (lane >= 64 - reach) & (lane < 64 + reach)
    for place in places:
        m = place_block(place, nblk, ring)
        v = jnp.where(m == 0, 0, jnp.where(m == nblk - 1, 2, 1))
        after = jnp.minimum(m + 1, nblk - 1)
        before = jnp.maximum(m - 1, 0)
        for s in range(3):

            def get(ref, i):
                return ref[i, 2 * s : 2 * s + 2].reshape(2 * rows, LANES)

            def rim(ref):
                return jnp.where(lane < 64, get(ref, after), get(ref, before))

            high, low, own = rim(rhi), rim(rlo), get(rhi, m)
            packed = jnp.where(in_low, pltpu.roll(low, 96, 1), jnp.where(in_high, pltpu.roll(high, 64, 1), high))
            q = dot(jnp.concatenate([own, get(rlo, m)], axis=1), wcol[v, s, 0])
            q = q + dot(jnp.concatenate([own, packed], axis=1), wcol[v, s, 1])
            for i in range(2):
                for j in range(2):
                    out[m, 4 * s + i + 2 * j] = q[i * rows : (i + 1) * rows, j * LANES : (j + 1) * LANES]


def final_kernel(system, d0, images, detection, coefficients, solved, out, scalars, sems):
    a = system[...]
    row = row_index(a.shape)
    col = [jnp.broadcast_to(a[:, j : j + 1], a.shape) for j in range(NB + 1)]
    trace = col[0][0:1, :]
    for k in range(1, NB):
        trace = trace + col[k][k : k + 1, :]
    ridge = trace * (0.05 / NB)
    for k in range(NB):
        col[k] = jnp.where(row == k, col[k] + ridge, col[k])
    result = jnp.zeros(a.shape, F32)
    for k in range(NB):
        factor = jnp.where(row == k, 0.0, col[k] * (1.0 / col[k][k : k + 1, :]))
        for j in range(k + 1, NB + 1):
            col[j] = col[j] - factor * col[j][k : k + 1, :]
    for k in range(NB):
        result = jnp.where(row == k, col[NB] / col[k], result)
    solved[...] = result
    for k in range(NB):
        scalars[k] = solved[k, 0]
    nblk, _, rows = images.shape[:3]
    parts = sems.shape[0] - 1
    size = rows // parts
    copies = [pltpu.make_async_copy(scalars, coefficients, sems.at[parts])]
    copies[0].start()
    for c in range(parts):
        piece = slice(c * size, (c + 1) * size)
        for m in range(nblk):
            total = d0[piece, m * LANES : (m + 1) * LANES]
            for k in range(NB):
                total = total - solved[k : k + 1, :] * images[m, k, piece, :]
            out[piece, m * LANES : (m + 1) * LANES] = total
        copies.append(pltpu.make_async_copy(out.at[piece], detection.at[piece], sems.at[c]))
        copies[-1].start()
    for copy in copies:
        copy.wait()


def ring_order(count):
    return list(range(0, count, 2)) + list(range(count - 1, 0, -2))


def swap(x):
    return lax.ppermute(x, "tile", [(0, 1), (1, 0)])


def gather_ring(block, count):
    ring = ring_order(count)
    ahead = [(ring[i], ring[(i + 1) % count]) for i in range(count)]
    back = [(t, s) for s, t in ahead]
    out = [block]
    fwd = bwd = block
    for step in range(count // 2):
        if step < count // 2 - 1:
            bwd = lax.ppermute(bwd, "epoch", back)
        fwd = lax.ppermute(fwd, "epoch", ahead)
        out += [fwd, bwd]
    return out[:count]


def all_sum(x, count, beside):
    beside[0](x)
    x = x + swap(x)
    if count & (count - 1):
        for f in beside[1:]:
            f(x)
        return lax.psum(x, "epoch")
    steps = count.bit_length() - 1
    for i in range(steps):
        for f in beside[1 + i :: steps]:
            f(x)
        x = x + lax.ppermute(x, "epoch", [(j, j ^ (1 << i)) for j in range(count)])
    return x


def in_vmem(x):
    return pltpu.with_memory_space_constraint(x, pltpu.VMEM)


ANY = functools.partial(pl.BlockSpec, memory_space=pl.ANY)
HBM = functools.partial(pl.BlockSpec, memory_space=pltpu.HBM)


def call(kernel, name, out, ins, limit, flops, scratch=(), aliases=None, outside=(), hbm=()):
    ins = [pltpu.with_memory_space_constraint(x, pltpu.HBM) if i in hbm else x for i, x in enumerate(ins)]

    def spec(i, x):
        if i in outside:
            return ANY()
        if i in hbm:
            return HBM()
        return SMEM() if x.ndim == 1 else VMEM()

    return pl.pallas_call(
        kernel,
        out_shape=out,
        in_specs=[spec(i, x) for i, x in enumerate(ins)],
        out_specs=jax.tree.map(lambda _: VMEM(), out, is_leaf=lambda x: hasattr(x, "shape")),
        scratch_shapes=scratch,
        input_output_aliases=aliases or {},
        compiler_params=pltpu.CompilerParams(vmem_limit_bytes=limit * 2**20),
        cost_estimate=pl.CostEstimate(flops=flops, bytes_accessed=2**20, transcendentals=0),
        name=name,
    )(*ins)


def local(template, science, flags, stamp_rows, stamp_cols):
    n_tile = lax.axis_size("tile")
    n_epoch = lax.axis_size("epoch")
    rows, width = template.shape
    science, flags = science[0], flags[0]
    cols = science.shape[1]
    nblk = cols // LANES
    nrow = rows // LANES
    stamps = stamp_rows.shape[1]
    groups = stamps // 4
    depth = groups * STAMP
    ring = width == LANES
    tile = lax.axis_index("tile")

    def edge_of(x):
        return jnp.where(tile == 0, x[-HALO:], x[:HALO])

    other = swap(template)
    tall = lax.optimization_barrier(jnp.pad(template, ((0, HALO), (0, 0))))
    tall = lax.dynamic_update_slice(tall, jnp.where(tile == 0, other[:HALO], other[-HALO:]), (rows, 0))
    _, later, stamp_rows, stamp_cols = lax.optimization_barrier((tall, science, stamp_rows, stamp_cols))
    science_edge = swap(edge_of(later))
    if ring:
        blocks = gather_ring(tall, n_epoch)
    else:
        whole = lax.all_gather(tall, "epoch", axis=1, tiled=True)
        blocks = [whole[:, m * LANES : (m + 1) * LANES] for m in range(nblk)]
    info = jnp.concatenate([stamp_rows[0], stamp_cols[0]])

    lrow6, lrow1 = (jnp.asarray(x) for x in row_tables())
    wcol6, wcol1 = (jnp.asarray(x) for x in column_tables())
    tables = [lrow1, wcol1]
    later_tables = [wcol6, jnp.asarray(stamp_table())]

    def like(xs):
        return tuple(pltpu.VMEM(x.shape, x.dtype) for x in xs)

    sci, bad, lrow6, lrow1, wcol1 = map(in_vmem, call(
        functools.partial(load_kernel, n_tile),
        "load",
        (
            pltpu.VMEM((nblk, rows, LANES), F32),
            pltpu.VMEM((nblk, rows, LANES), jnp.int32),
            pltpu.VMEM((nrow,) + lrow6.shape[1:], BF16),
        )
        + like(tables),
        [tall, science, flags, lrow6] + tables,
        2,
        2 * 10**9,
        [pltpu.SemaphoreType.DMA((2 * nblk + nrow + len(tables),))],
        outside=(0,),
        hbm=range(1, 4 + len(tables)),
    ))
    d0, wcol6, mcol = map(in_vmem, call(
        functools.partial(science_kernel, n_tile),
        "science_filter",
        (pltpu.VMEM((rows, cols), F32),) + like(later_tables),
        [sci, science_edge, lrow1, wcol1, blocks[1]] + later_tables,
        12,
        2 * 10**9,
        [pltpu.VMEM((nblk, rows, LANES), F32), pltpu.SemaphoreType.DMA((len(later_tables),))],
        outside=(4,),
        hbm=range(5, 5 + len(later_tables)),
    ))
    wp, sp = map(in_vmem, call(
        cut_kernel,
        "stamp_pixels",
        (pltpu.VMEM((depth, LANES), F32),) * 2,
        [info, sci, bad, blocks[3]],
        4,
        10**9,
        outside=(3,),
    ))

    def row_filters(slots, r, store):
        ins = [lrow6, blocks[1] if store else d0] + [blocks[slot] for slot in slots]
        n = len(ins)
        out = (pltpu.VMEM((nblk, 6, rows, LANES), BF16),) * 2
        if store:
            out += (pltpu.VMEM((nblk + 2, rows + 2 * HALO, LANES), F32),)
        return call(
            functools.partial(rows_kernel, n_tile, slots, ring, store),
            "template_rows",
            out,
            ins + [in_vmem(x) for x in r],
            12,
            10**9,
            aliases={n + i: i for i in range(len(r))},
            outside=(1,),
        )

    def column_filters(places, r, q, after):
        ins = [in_vmem(x) for x in r] + [wcol6, after] + [in_vmem(x) for x in q]
        return call(
            functools.partial(columns_kernel, nblk, places, ring),
            "template_columns",
            pltpu.VMEM((nblk, NB, rows, LANES), F32),
            ins,
            12,
            5 * 10**7 * len(places),
            aliases={4: 0} if q else None,
            outside=(3,),
        )

    r = ()
    for slots in [(0,)] + [(i, i + 1) for i in range(1, nblk - 1, 2)]:
        r = row_filters(slots, r, True)
    padded = r[2]
    state = dict(r=r[:2], q=())

    def more_columns(places):
        def go(x):
            state["q"] = (column_filters(places, state["r"], state["q"], x),)

        return go

    def last_rows(x):
        state["r"] = row_filters((nblk - 1,), state["r"], False)

    more_columns(range(nblk - 4))(blocks[-2])

    system, _ = call(
        functools.partial(stamp_kernel, n_tile, nblk, ring),
        "stamp_sums",
        (pltpu.VMEM((16, LANES), F32), pltpu.VMEM(padded.shape, F32)),
        [info, blocks[-1], in_vmem(padded), wp, sp, mcol, in_vmem(state["q"][0])],
        12,
        10**9,
        [
            pltpu.VMEM((6, groups * PATCH_ROWS, LANES), F32),
            pltpu.VMEM((NB, depth, LANES), F32),
        ],
        aliases={2: 1},
        outside=(6,),
    )
    beside = [last_rows] + [more_columns(range(i, i + 2)) for i in range(nblk - 4, nblk, 2)]
    system = all_sum(system, n_epoch, beside)

    parts = 8
    detection, coefficients = pl.pallas_call(
        final_kernel,
        out_shape=(
            jax.ShapeDtypeStruct((rows, cols), F32),
            jax.ShapeDtypeStruct((NB,), F32),
        ),
        in_specs=[VMEM()] * 3,
        out_specs=(HBM(), HBM()),
        scratch_shapes=[
            pltpu.VMEM((16, LANES), F32),
            pltpu.VMEM((rows, cols), F32),
            pltpu.SMEM((NB,), F32),
            pltpu.SemaphoreType.DMA((parts + 1,)),
        ],
        compiler_params=pltpu.CompilerParams(vmem_limit_bytes=8 * 2**20),
        cost_estimate=pl.CostEstimate(flops=10**8, bytes_accessed=16 * 2**20, transcendentals=0),
        name="solve_subtract",
    )(system, d0, in_vmem(state["q"][0]))
    return (detection[None], coefficients)


def solution(mesh):
    return jax.shard_map(
        local,
        mesh=mesh,
        in_specs=(
            P(("patch", "tile"), "epoch"),
            P(("patch", "epoch"), "tile", None),
            P(("patch", "epoch"), "tile", None),
            P(("patch", "epoch"), "tile"),
            P(("patch", "epoch"), "tile"),
        ),
        out_specs=(P(("patch", "epoch"), "tile", None), P("patch")),
        check_vma=False,
    )
```

```python
import functools

import jax
import jax.numpy as jnp
import numpy as np
from jax import lax
from jax.experimental import pallas as pl
from jax.experimental.pallas import tpu as pltpu
from jax.sharding import PartitionSpec as P

STAMP = 32
HALF = 7
TAPS = 15
SIGMAS = (1.0, 2.0, 3.5)
NB = 12
LANES = 128
HALO = 16
WIN = LANES + 2 * HALO
PATCH_ROWS = 48
F32 = jnp.float32
BF16 = jnp.bfloat16
LIMIT = 56 * 1024 * 1024


def split_np(a):
    a = np.asarray(a, np.float32)
    hi = a.astype(BF16)
    lo = (a - hi.astype(np.float32)).astype(BF16)
    return hi, lo


def profiles():
    offsets = np.arange(TAPS, dtype=np.float64) - HALF
    rows = []
    for sigma in SIGMAS:
        gauss = np.exp(-offsets * offsets / (2.0 * sigma * sigma))
        gauss = gauss / gauss.sum()
        rows += [gauss, gauss * offsets / HALF]
    return np.stack(rows)


def psf_profile():
    offsets = np.arange(TAPS, dtype=np.float64) - HALF
    gauss = np.exp(-offsets * offsets / 4.5)
    return gauss / gauss.sum()


def band(profile, size):
    out = np.zeros((size, size))
    for shift in range(TAPS):
        out += profile[shift] * np.eye(size, k=shift - HALF)
    return out


def three_bands(size):
    psf = band(psf_profile(), size)
    return [psf @ band(p, size) for p in profiles()], psf


def pick(matrix, rows, cols):
    cols = np.asarray(cols)
    ok = (cols >= 0) & (cols < matrix.shape[1])
    out = matrix[np.asarray(rows)[:, None], np.clip(cols, 0, matrix.shape[1] - 1)[None, :]]
    return np.where(ok[None, :], out, 0.0)


def starts():
    return (0, LANES, 2 * LANES)


def row_tables():
    size = 3 * LANES
    ops, psf = three_bands(size)

    def stack(ms):
        out = []
        for start in starts():
            rows = np.arange(LANES) + start
            cols = np.arange(WIN) + start - HALO
            hi, lo = split_np(np.concatenate([pick(m, rows, cols) for m in ms], axis=0))
            out.append(np.concatenate([hi, hi, lo], axis=1))
        return np.stack(out)

    return stack(ops), stack([psf])


def column_tables():
    size = 3 * LANES
    ops, psf = three_bands(size)
    lane = np.arange(LANES)

    def own(matrix, start):
        return split_np(pick(matrix, lane + start, lane + start).T)

    def rim(matrix, start):
        side = np.where(lane < 64, start + LANES + lane, start - LANES + lane)
        return split_np(pick(matrix, lane + start, side).T)

    def model(matrix, start):
        hi, lo = own(matrix, start)
        rhi, rlo = rim(matrix, start)
        packed = np.zeros_like(rhi)
        for at in list(range(2 * HALF)) + list(range(LANES - 2 * HALF, LANES)):
            packed[at] = rhi[at]
            packed[(at + 64) % LANES] = rlo[at]
            packed[(at + 96) % LANES] = rhi[at]
        return np.stack([np.concatenate([hi, hi]), np.concatenate([lo, packed])])

    def science(start):
        return np.stack([np.concatenate(p) for p in zip(own(psf, start), rim(psf, start))])

    models = [
        [np.concatenate([model(ops[2 * s], start), model(ops[2 * s + 1], start)], axis=2) for s in range(3)]
        for start in starts()
    ]
    return np.array(models), np.stack([science(start) for start in starts()])


def stamp_table():
    prof = profiles()
    out = np.zeros((256, 6, LANES))
    for q in range(4):
        for c in range(STAMP):
            for v in range(TAPS):
                out[q * 64 + c + v, :, q * STAMP + c] = prof[:, v]
    return np.stack(split_np(out.reshape(256, 6 * LANES)))


def dot(a, b):
    return jnp.dot(a, b, preferred_element_type=F32)


def split(x):
    hi = x.astype(BF16)
    lo = (x - hi.astype(F32)).astype(BF16)
    return hi, lo


def stack3(x):
    hi, lo = split(x)
    return jnp.concatenate([hi, lo, hi], axis=0)


def params(**kw):
    return pltpu.CompilerParams(vmem_limit_bytes=LIMIT, **kw)


VMEM = functools.partial(pl.BlockSpec, memory_space=pltpu.VMEM)
SMEM = functools.partial(pl.BlockSpec, memory_space=pltpu.SMEM)


def row_index(shape):
    return lax.broadcasted_iota(jnp.int32, shape, len(shape) - 2)


def lane_index(shape):
    return lax.broadcasted_iota(jnp.int32, shape, len(shape) - 1)


def ring_place(step, count):
    me = lax.axis_index("epoch")
    at = jnp.where(lax.rem(me, 2) == 0, me // 2, count - 1 - me // 2)
    at = lax.rem(at + step + count, count)
    return jnp.where(at < count // 2, 2 * at, 2 * (count - 1 - at) + 1)


def slot_block(slot, nblk, ring):
    if not ring:
        return jnp.int32(slot)
    step = (slot + 1) // 2
    return ring_place(step if slot % 2 == 0 else -step, nblk)


def place_block(place, nblk, ring):
    return lax.rem(slot_block(nblk - 1, nblk, ring) + 2 + place, nblk)


def variant(tile, b, n_tile, nrow):
    v = jnp.int32(1)
    if b == 0:
        v = jnp.where(tile == 0, 0, v)
    if b == nrow - 1:
        v = jnp.where(tile == n_tile - 1, 2, v)
    return v


def window_rows(tile, b, n_tile, nrow, own, edge):
    size = nrow * LANES
    low, high = b * LANES - HALO, (b + 1) * LANES + HALO
    parts = []
    if low < 0:
        parts.append(jnp.where(tile == 0, 0.0, edge()))
    parts.append(own(max(low, 0), min(high, size)))
    if high > size:
        parts.append(jnp.where(tile == n_tile - 1, 0.0, edge()))
    return jnp.concatenate(parts, axis=0)


def science_kernel(n_tile, sci, edge, lrow, wcol, after, *refs):
    count = len(refs) // 2 - 1
    d0, mid, sems = refs[count], refs[-2], refs[-1]
    copies = [pltpu.make_async_copy(refs[i], refs[count + 1 + i], sems.at[i]) for i in range(count)]
    for copy in copies:
        copy.start()
    tile = lax.axis_index("tile")
    nblk, rows = sci.shape[:2]
    nrow = rows // LANES
    for b in range(nrow):
        left = lrow[variant(tile, b, n_tile, nrow)]
        for m in range(0, nblk, 2):

            def own(lo, hi):
                return jnp.concatenate([sci[m, lo:hi, :], sci[m + 1, lo:hi, :]], axis=1)

            x = window_rows(tile, b, n_tile, nrow, own, lambda: edge[:, m * LANES : (m + 2) * LANES])
            y = dot(left, stack3(x))
            mid[m, b * LANES : (b + 1) * LANES, :] = y[:, :LANES]
            mid[m + 1, b * LANES : (b + 1) * LANES, :] = y[:, LANES:]
    lane = lane_index((rows, LANES))
    for m in range(nblk):
        v = 0 if m == 0 else (2 if m == nblk - 1 else 1)
        rim = jnp.where(lane < 64, mid[min(m + 1, nblk - 1)], mid[max(m - 1, 0)])
        hi, lo = split(jnp.concatenate([mid[m], rim], axis=1))
        d0[:, m * LANES : (m + 1) * LANES] = dot(hi, wcol[v, 0]) + dot(lo, wcol[v, 0]) + dot(hi, wcol[v, 1])
    for copy in copies:
        copy.wait()


def load_kernel(n_tile, *refs):
    half = len(refs) // 2
    after, sci, flags, lrow, *tables = refs[:half]
    sb, fb, lout, *outs = refs[half:-1]
    sems = refs[-1]
    tile = lax.axis_index("tile")
    nblk, rows = sb.shape[:2]
    nrow = rows // LANES
    pairs = []
    for m in range(nblk):
        piece = slice(m * LANES, (m + 1) * LANES)
        pairs += [(sci.at[:, piece], sb.at[m]), (flags.at[:, piece], fb.at[m])]
    pairs += [(lrow.at[variant(tile, b, n_tile, nrow)], lout.at[b]) for b in range(nrow)]
    pairs += list(zip(tables, outs))
    copies = [pltpu.make_async_copy(a, b, sems.at[i]) for i, (a, b) in enumerate(pairs)]
    for copy in copies:
        copy.start()
    for copy in copies:
        copy.wait()


def cut_kernel(info, sb, fb, after, wp, sp, places):
    stamps = info.shape[0] // 2
    nblk = sb.shape[0]
    for i in range(2 * stamps):
        places[i] = info[i]
    lane = lane_index((STAMP, LANES))
    for g in range(stamps // 4):
        w = jnp.zeros((STAMP, LANES), F32)
        s = jnp.zeros((STAMP, LANES), F32)
        for q in range(4):
            top = info[g * 4 + q]
            left = info[stamps + g * 4 + q]
            blk = left // LANES
            off = left - blk * LANES
            nxt = jnp.minimum(blk + 1, nblk - 1)
            shift = lax.rem(q * STAMP - off + LANES, LANES)
            near = lane < q * STAMP - off + LANES
            here = (lane >= q * STAMP) & (lane < (q + 1) * STAMP)

            def window(ref):
                a = pltpu.roll(ref[blk, pl.ds(top, STAMP), :], shift, 1)
                b = pltpu.roll(ref[nxt, pl.ds(top, STAMP), :], shift, 1)
                return jnp.where(near, a, b)

            w = jnp.where(here & (window(fb) == 0), 1.0, w)
            s = jnp.where(here, window(sb), s)
        wp[g * STAMP : (g + 1) * STAMP, :] = w
        sp[g * STAMP : (g + 1) * STAMP, :] = jnp.where(w > 0.0, s, 0.0)


def put_block(n_tile, block, at, t):
    tile = lax.axis_index("tile")
    rows = block.shape[0] - HALO
    e = block[rows:, :]
    t[at + 1, 0:HALO, :] = jnp.where(tile == 0, 0.0, e)
    t[at + 1, HALO : HALO + rows, :] = block[0:rows, :]
    t[at + 1, HALO + rows :, :] = jnp.where(tile == n_tile - 1, 0.0, e)


def stamp_kernel(n_tile, nblk, ring, info, last, t_in, wp, sp, mcol, after, system, t, y, images):
    stamps = info.shape[0] // 2
    put_block(n_tile, last, slot_block(nblk - 1, nblk, ring), t)
    groups = stamps // 4
    lane = lane_index((PATCH_ROWS, LANES))
    prof = profiles()
    xs = []
    for g in range(groups):
        halves = []
        for pair in range(2):
            parts = []
            for h in range(2):
                j = g * 4 + pair * 2 + h
                start = info[stamps + j] + (LANES - HALF)
                blk = start // LANES
                off = start - blk * LANES
                shift = lax.rem(64 * h - off + LANES, LANES)
                rows = pl.ds(info[j] + (HALO - HALF), PATCH_ROWS)
                a = pltpu.roll(t[blk, rows, :], shift, 1)
                b = pltpu.roll(t[blk + 1, rows, :], shift, 1)
                parts.append(jnp.where(lane < 64 * h - off + LANES, a, b))
            halves.append(jnp.where(lane < 64, parts[0], parts[1]))
        xs.append(jnp.concatenate(halves, axis=1))
    hi, lo = split(jnp.concatenate(xs, axis=0))
    both = jnp.concatenate([hi, lo], axis=0)
    depth = groups * PATCH_ROWS
    for p in range(0, 6, 2):
        piece = slice(p * LANES, (p + 2) * LANES)
        main = dot(both, mcol[0, :, piece])
        total = main[:depth] + main[depth:] + dot(hi, mcol[1, :, piece])
        y[p] = total[:, :LANES]
        y[p + 1] = total[:, LANES:]
    for s in range(3):
        gauss = prof[2 * s]
        for j in range(2):
            for g in range(groups):
                base = g * PATCH_ROWS

                def at(o):
                    return y[2 * s + j, base + HALF + o : base + HALF + o + STAMP, :]

                even = at(0) * np.float32(gauss[HALF])
                odd = None
                for d in range(1, HALF + 1):
                    up, down = at(d), at(-d)
                    even = even + (up + down) * np.float32(gauss[HALF + d])
                    term = (up - down) * np.float32(gauss[HALF + d] * d / HALF)
                    odd = term if odd is None else odd + term
                images[4 * s + 2 * j, g * STAMP : (g + 1) * STAMP, :] = even
                images[4 * s + 2 * j + 1, g * STAMP : (g + 1) * STAMP, :] = odd
    depth = groups * STAMP
    row = row_index((8, LANES))
    lane = lane_index((8, LANES))
    zero = jnp.zeros((8, LANES), F32)
    tiles = [[zero, zero] for _ in range(NB + 1)]

    def collect(k, l, x):
        tiles[l][k // 8] = jnp.where(row == k % 8, x, tiles[l][k // 8])

    w = wp[...]
    for k in range(NB):
        weighted = w * images[k]
        for l in range(k, NB + 1):
            prod = weighted * images[l] if l < NB else sp[...] * images[k]
            x = jnp.sum(prod.reshape(depth // 8, 8, LANES), axis=0)
            for d in (4, 2, 1):
                x = x + pltpu.roll(x, d, 0)
            collect(k, l, x)
            if k < l < NB:
                collect(l, k, x)
    for h in range(2):
        out = zero
        for l in range(NB + 1):
            out = jnp.where(lane == l, jnp.sum(tiles[l][h], axis=1, keepdims=True), out)
        system[h * 8 : (h + 1) * 8, :] = out


def rows_kernel(n_tile, slots, ring, store, lrow, after, *refs):
    blocks = refs[: len(slots)]
    rhi, rlo = refs[-3:-1] if store else refs[-2:]
    tile = lax.axis_index("tile")
    nblk, _, rows = rhi.shape[:3]
    nrow = rows // LANES
    places = [slot_block(slot, nblk, ring) for slot in slots]
    if store:
        t = refs[-1]
        if slots[0] == 0:
            t[0] = jnp.zeros(t.shape[1:], F32)
            t[nblk + 1] = jnp.zeros(t.shape[1:], F32)
        for block, at in zip(blocks, places):
            put_block(n_tile, block, at, t)
    for b in range(nrow):
        xs = [
            window_rows(tile, b, n_tile, nrow, lambda lo, hi: block[lo:hi, :], lambda: block[rows:, :])
            for block in blocks
        ]
        hi, lo = split(dot(lrow[b], stack3(jnp.concatenate(xs, axis=1) if len(xs) > 1 else xs[0])))
        for h, at in enumerate(places):
            for p in range(6):
                piece = (slice(p * LANES, (p + 1) * LANES), slice(h * LANES, (h + 1) * LANES))
                rhi[at, p, b * LANES : (b + 1) * LANES, :] = hi[piece]
                rlo[at, p, b * LANES : (b + 1) * LANES, :] = lo[piece]


def columns_kernel(nblk, places, ring, rhi, rlo, wcol, after, *refs):
    out = refs[-1]
    rows = rhi.shape[2]
    lane = lane_index((2 * rows, LANES))
    reach = 2 * HALF
    in_low = (lane >= 96 - reach) & (lane < 96 + reach)
    in_high = (lane >= 64 - reach) & (lane < 64 + reach)
    for place in places:
        m = place_block(place, nblk, ring)
        v = jnp.where(m == 0, 0, jnp.where(m == nblk - 1, 2, 1))
        after = jnp.minimum(m + 1, nblk - 1)
        before = jnp.maximum(m - 1, 0)
        for s in range(3):

            def get(ref, i):
                return ref[i, 2 * s : 2 * s + 2].reshape(2 * rows, LANES)

            def rim(ref):
                return jnp.where(lane < 64, get(ref, after), get(ref, before))

            high, low, own = rim(rhi), rim(rlo), get(rhi, m)
            packed = jnp.where(in_low, pltpu.roll(low, 96, 1), jnp.where(in_high, pltpu.roll(high, 64, 1), high))
            q = dot(jnp.concatenate([own, get(rlo, m)], axis=1), wcol[v, s, 0])
            q = q + dot(jnp.concatenate([own, packed], axis=1), wcol[v, s, 1])
            for i in range(2):
                for j in range(2):
                    out[m, 4 * s + i + 2 * j] = q[i * rows : (i + 1) * rows, j * LANES : (j + 1) * LANES]


def final_kernel(system, d0, images, detection, coefficients, solved, out, scalars, sems):
    a = system[...]
    row = row_index(a.shape)
    col = [jnp.broadcast_to(a[:, j : j + 1], a.shape) for j in range(NB + 1)]
    trace = col[0][0:1, :]
    for k in range(1, NB):
        trace = trace + col[k][k : k + 1, :]
    ridge = trace * (0.05 / NB)
    for k in range(NB):
        col[k] = jnp.where(row == k, col[k] + ridge, col[k])
    result = jnp.zeros(a.shape, F32)
    for k in range(NB):
        factor = jnp.where(row == k, 0.0, col[k] * (1.0 / col[k][k : k + 1, :]))
        for j in range(k + 1, NB + 1):
            col[j] = col[j] - factor * col[j][k : k + 1, :]
    for k in range(NB):
        result = jnp.where(row == k, col[NB] / col[k], result)
    solved[...] = result
    for k in range(NB):
        scalars[k] = solved[k, 0]
    nblk, _, rows = images.shape[:3]
    parts = sems.shape[0] - 1
    size = rows // parts
    copies = [pltpu.make_async_copy(scalars, coefficients, sems.at[parts])]
    copies[0].start()
    for c in range(parts):
        piece = slice(c * size, (c + 1) * size)
        for m in range(nblk):
            total = d0[piece, m * LANES : (m + 1) * LANES]
            for k in range(NB):
                total = total - solved[k : k + 1, :] * images[m, k, piece, :]
            out[piece, m * LANES : (m + 1) * LANES] = total
        copies.append(pltpu.make_async_copy(out.at[piece], detection.at[piece], sems.at[c]))
        copies[-1].start()
    for copy in copies:
        copy.wait()


def ring_order(count):
    return list(range(0, count, 2)) + list(range(count - 1, 0, -2))


def swap(x):
    return lax.ppermute(x, "tile", [(0, 1), (1, 0)])


def gather_ring(block, count):
    ring = ring_order(count)
    ahead = [(ring[i], ring[(i + 1) % count]) for i in range(count)]
    back = [(t, s) for s, t in ahead]
    out = [block]
    fwd = bwd = block
    for step in range(count // 2):
        if step < count // 2 - 1:
            bwd = lax.ppermute(bwd, "epoch", back)
        fwd = lax.ppermute(fwd, "epoch", ahead)
        out += [fwd, bwd]
    return out[:count]


def all_sum(x, count, beside):
    beside[0](x)
    x = x + swap(x)
    if count & (count - 1) or count < 4:
        for f in beside[1:]:
            f(x)
        return lax.psum(x, "epoch")

    def other(bits):
        return lax.ppermute(x, "epoch", [(j, j ^ bits) for j in range(count)])

    beside[1](x)
    x = (x + other(1)) + (other(2) + other(3))
    bit = 4
    for f in beside[2:]:
        f(x)
    while bit < count:
        x = x + other(bit)
        bit *= 2
    return x


def in_vmem(x):
    return pltpu.with_memory_space_constraint(x, pltpu.VMEM)


ANY = functools.partial(pl.BlockSpec, memory_space=pl.ANY)
HBM = functools.partial(pl.BlockSpec, memory_space=pltpu.HBM)


def call(kernel, name, out, ins, limit, flops, scratch=(), aliases=None, outside=(), hbm=()):
    ins = [pltpu.with_memory_space_constraint(x, pltpu.HBM) if i in hbm else x for i, x in enumerate(ins)]

    def spec(i, x):
        if i in outside:
            return ANY()
        if i in hbm:
            return HBM()
        return SMEM() if x.ndim == 1 else VMEM()

    return pl.pallas_call(
        kernel,
        out_shape=out,
        in_specs=[spec(i, x) for i, x in enumerate(ins)],
        out_specs=jax.tree.map(lambda x: SMEM() if len(x.shape) == 1 else VMEM(), out, is_leaf=lambda x: hasattr(x, "shape")),
        scratch_shapes=scratch,
        input_output_aliases=aliases or {},
        compiler_params=pltpu.CompilerParams(vmem_limit_bytes=limit * 2**20),
        cost_estimate=pl.CostEstimate(flops=flops, bytes_accessed=2**20, transcendentals=0),
        name=name,
    )(*ins)


def local(template, science, flags, stamp_rows, stamp_cols):
    n_tile = lax.axis_size("tile")
    n_epoch = lax.axis_size("epoch")
    rows, width = template.shape
    science, flags = science[0], flags[0]
    cols = science.shape[1]
    nblk = cols // LANES
    nrow = rows // LANES
    stamps = stamp_rows.shape[1]
    groups = stamps // 4
    depth = groups * STAMP
    ring = width == LANES
    tile = lax.axis_index("tile")

    def edge_of(x):
        return jnp.where(tile == 0, x[-HALO:], x[:HALO])

    other = swap(template)
    tall = lax.optimization_barrier(jnp.pad(template, ((0, HALO), (0, 0))))
    tall = lax.dynamic_update_slice(tall, jnp.where(tile == 0, other[:HALO], other[-HALO:]), (rows, 0))
    _, later, stamp_rows, stamp_cols = lax.optimization_barrier((tall, science, stamp_rows, stamp_cols))
    science_edge = swap(edge_of(later))
    if ring:
        blocks = gather_ring(tall, n_epoch)
    else:
        whole = lax.all_gather(tall, "epoch", axis=1, tiled=True)
        blocks = [whole[:, m * LANES : (m + 1) * LANES] for m in range(nblk)]
    info = jnp.concatenate([stamp_rows[0], stamp_cols[0]])

    lrow6, lrow1 = (jnp.asarray(x) for x in row_tables())
    wcol6, wcol1 = (jnp.asarray(x) for x in column_tables())
    tables = [lrow1, wcol1]
    later_tables = [wcol6, jnp.asarray(stamp_table())]

    def like(xs):
        return tuple(pltpu.VMEM(x.shape, x.dtype) for x in xs)

    sci, bad, lrow6, lrow1, wcol1 = map(in_vmem, call(
        functools.partial(load_kernel, n_tile),
        "load",
        (
            pltpu.VMEM((nblk, rows, LANES), F32),
            pltpu.VMEM((nblk, rows, LANES), jnp.int32),
            pltpu.VMEM((nrow,) + lrow6.shape[1:], BF16),
        )
        + like(tables),
        [tall, science, flags, lrow6] + tables,
        2,
        2 * 10**9,
        [pltpu.SemaphoreType.DMA((2 * nblk + nrow + len(tables),))],
        outside=(0,),
        hbm=range(1, 4 + len(tables)),
    ))
    d0, wcol6, mcol = map(in_vmem, call(
        functools.partial(science_kernel, n_tile),
        "science_filter",
        (pltpu.VMEM((rows, cols), F32),) + like(later_tables),
        [sci, science_edge, lrow1, wcol1, blocks[1]] + later_tables,
        12,
        2 * 10**9,
        [pltpu.VMEM((nblk, rows, LANES), F32), pltpu.SemaphoreType.DMA((len(later_tables),))],
        outside=(4,),
        hbm=range(5, 5 + len(later_tables)),
    ))
    wp, sp, info = call(
        cut_kernel,
        "stamp_pixels",
        (pltpu.VMEM((depth, LANES), F32),) * 2 + (pltpu.SMEM(info.shape, info.dtype),),
        [info, sci, bad, blocks[3]],
        4,
        10**9,
        outside=(3,),
    )
    wp, sp = in_vmem(wp), in_vmem(sp)
    info = pltpu.with_memory_space_constraint(info, pltpu.SMEM)

    def row_filters(slots, r, store):
        ins = [lrow6, blocks[1] if store else d0] + [blocks[slot] for slot in slots]
        n = len(ins)
        out = (pltpu.VMEM((nblk, 6, rows, LANES), BF16),) * 2
        if store:
            out += (pltpu.VMEM((nblk + 2, rows + 2 * HALO, LANES), F32),)
        return call(
            functools.partial(rows_kernel, n_tile, slots, ring, store),
            "template_rows",
            out,
            ins + [in_vmem(x) for x in r],
            12,
            10**9,
            aliases={n + i: i for i in range(len(r))},
            outside=(1,),
        )

    def column_filters(places, r, q, after):
        ins = [in_vmem(x) for x in r] + [wcol6, after] + [in_vmem(x) for x in q]
        return call(
            functools.partial(columns_kernel, nblk, places, ring),
            "template_columns",
            pltpu.VMEM((nblk, NB, rows, LANES), F32),
            ins,
            12,
            5 * 10**7 * len(places),
            aliases={4: 0} if q else None,
            outside=(3,),
        )

    r = ()
    for slots in [(0,)] + [(i, i + 1) for i in range(1, nblk - 1, 2)]:
        r = row_filters(slots, r, True)
    padded = r[2]
    state = dict(r=r[:2], q=())

    def more_columns(places):
        def go(x):
            state["q"] = (column_filters(places, state["r"], state["q"], x),)

        return go

    def last_rows(x):
        state["r"] = row_filters((nblk - 1,), state["r"], False)

    more_columns(range(nblk - 4))(blocks[-2])

    system, _ = call(
        functools.partial(stamp_kernel, n_tile, nblk, ring),
        "stamp_sums",
        (pltpu.VMEM((16, LANES), F32), pltpu.VMEM(padded.shape, F32)),
        [info, blocks[-1], in_vmem(padded), wp, sp, mcol, in_vmem(state["q"][0])],
        12,
        10**9,
        [
            pltpu.VMEM((6, groups * PATCH_ROWS, LANES), F32),
            pltpu.VMEM((NB, depth, LANES), F32),
        ],
        aliases={2: 1},
        outside=(6,),
    )
    beside = [last_rows] + [more_columns(range(i, i + 2)) for i in range(nblk - 4, nblk, 2)]
    system = all_sum(system, n_epoch, beside)

    parts = 8
    detection, coefficients = pl.pallas_call(
        final_kernel,
        out_shape=(
            jax.ShapeDtypeStruct((rows, cols), F32),
            jax.ShapeDtypeStruct((NB,), F32),
        ),
        in_specs=[VMEM()] * 3,
        out_specs=(HBM(), HBM()),
        scratch_shapes=[
            pltpu.VMEM((16, LANES), F32),
            pltpu.VMEM((rows, cols), F32),
            pltpu.SMEM((NB,), F32),
            pltpu.SemaphoreType.DMA((parts + 1,)),
        ],
        compiler_params=pltpu.CompilerParams(vmem_limit_bytes=8 * 2**20),
        cost_estimate=pl.CostEstimate(flops=10**8, bytes_accessed=16 * 2**20, transcendentals=0),
        name="solve_subtract",
    )(system, d0, in_vmem(state["q"][0]))
    return (detection[None], coefficients)


def solution(mesh):
    return jax.shard_map(
        local,
        mesh=mesh,
        in_specs=(
            P(("patch", "tile"), "epoch"),
            P(("patch", "epoch"), "tile", None),
            P(("patch", "epoch"), "tile", None),
            P(("patch", "epoch"), "tile"),
            P(("patch", "epoch"), "tile"),
        ),
        out_specs=(P(("patch", "epoch"), "tile", None), P("patch")),
        check_vma=False,
    )
```

```python
import functools

import jax
import jax.numpy as jnp
import numpy as np
from jax import lax
from jax.experimental import pallas as pl
from jax.experimental.pallas import tpu as pltpu
from jax.sharding import PartitionSpec as P

STAMP = 32
HALF = 7
TAPS = 15
SIGMAS = (1.0, 2.0, 3.5)
NB = 12
LANES = 128
HALO = 16
WIN = LANES + 2 * HALO
PATCH_ROWS = 48
F32 = jnp.float32
BF16 = jnp.bfloat16
LIMIT = 56 * 1024 * 1024


def split_np(a):
    a = np.asarray(a, np.float32)
    hi = a.astype(BF16)
    lo = (a - hi.astype(np.float32)).astype(BF16)
    return hi, lo


def profiles():
    offsets = np.arange(TAPS, dtype=np.float64) - HALF
    rows = []
    for sigma in SIGMAS:
        gauss = np.exp(-offsets * offsets / (2.0 * sigma * sigma))
        gauss = gauss / gauss.sum()
        rows += [gauss, gauss * offsets / HALF]
    return np.stack(rows)


def psf_profile():
    offsets = np.arange(TAPS, dtype=np.float64) - HALF
    gauss = np.exp(-offsets * offsets / 4.5)
    return gauss / gauss.sum()


def band(profile, size):
    out = np.zeros((size, size))
    for shift in range(TAPS):
        out += profile[shift] * np.eye(size, k=shift - HALF)
    return out


def three_bands(size):
    psf = band(psf_profile(), size)
    return [psf @ band(p, size) for p in profiles()], psf


def pick(matrix, rows, cols):
    cols = np.asarray(cols)
    ok = (cols >= 0) & (cols < matrix.shape[1])
    out = matrix[np.asarray(rows)[:, None], np.clip(cols, 0, matrix.shape[1] - 1)[None, :]]
    return np.where(ok[None, :], out, 0.0)


def starts():
    return (0, LANES, 2 * LANES)


def row_tables():
    size = 3 * LANES
    ops, psf = three_bands(size)

    def stack(ms):
        out = []
        for start in starts():
            rows = np.arange(LANES) + start
            cols = np.arange(WIN) + start - HALO
            hi, lo = split_np(np.concatenate([pick(m, rows, cols) for m in ms], axis=0))
            out.append(np.concatenate([hi, hi, lo], axis=1))
        return np.stack(out)

    return stack(ops), stack([psf])


def column_tables():
    size = 3 * LANES
    ops, psf = three_bands(size)
    lane = np.arange(LANES)

    def own(matrix, start):
        return split_np(pick(matrix, lane + start, lane + start).T)

    def rim(matrix, start):
        side = np.where(lane < 64, start + LANES + lane, start - LANES + lane)
        return split_np(pick(matrix, lane + start, side).T)

    def model(matrix, start):
        hi, lo = own(matrix, start)
        rhi, rlo = rim(matrix, start)
        packed = np.zeros_like(rhi)
        for at in list(range(2 * HALF)) + list(range(LANES - 2 * HALF, LANES)):
            packed[at] = rhi[at]
            packed[(at + 64) % LANES] = rlo[at]
            packed[(at + 96) % LANES] = rhi[at]
        return np.stack([np.concatenate([hi, hi]), np.concatenate([lo, packed])])

    def science(start):
        return np.stack([np.concatenate(p) for p in zip(own(psf, start), rim(psf, start))])

    models = [
        [np.concatenate([model(ops[2 * s], start), model(ops[2 * s + 1], start)], axis=2) for s in range(3)]
        for start in starts()
    ]
    return np.array(models), np.stack([science(start) for start in starts()])


def stamp_table():
    prof = profiles()
    out = np.zeros((256, 6, LANES))
    for q in range(4):
        for c in range(STAMP):
            for v in range(TAPS):
                out[q * 64 + c + v, :, q * STAMP + c] = prof[:, v]
    return np.stack(split_np(out.reshape(256, 6 * LANES)))


def dot(a, b):
    return jnp.dot(a, b, preferred_element_type=F32)


def split(x):
    hi = x.astype(BF16)
    lo = (x - hi.astype(F32)).astype(BF16)
    return hi, lo


def stack3(x):
    hi, lo = split(x)
    return jnp.concatenate([hi, lo, hi], axis=0)


def params(**kw):
    return pltpu.CompilerParams(vmem_limit_bytes=LIMIT, **kw)


VMEM = functools.partial(pl.BlockSpec, memory_space=pltpu.VMEM)
SMEM = functools.partial(pl.BlockSpec, memory_space=pltpu.SMEM)


def row_index(shape):
    return lax.broadcasted_iota(jnp.int32, shape, len(shape) - 2)


def lane_index(shape):
    return lax.broadcasted_iota(jnp.int32, shape, len(shape) - 1)


def ring_place(step, count):
    me = lax.axis_index("epoch")
    at = jnp.where(lax.rem(me, 2) == 0, me // 2, count - 1 - me // 2)
    at = lax.rem(at + step + count, count)
    return jnp.where(at < count // 2, 2 * at, 2 * (count - 1 - at) + 1)


def slot_block(slot, nblk, ring):
    if not ring:
        return jnp.int32(slot)
    step = (slot + 1) // 2
    return ring_place(-step if slot % 2 == 0 else step, nblk)


def place_block(place, nblk, ring):
    return lax.rem(slot_block(nblk - 1, nblk, ring) + 2 + place, nblk)


def variant(tile, b, n_tile, nrow):
    v = jnp.int32(1)
    if b == 0:
        v = jnp.where(tile == 0, 0, v)
    if b == nrow - 1:
        v = jnp.where(tile == n_tile - 1, 2, v)
    return v


def window_rows(tile, b, n_tile, nrow, own, edge):
    size = nrow * LANES
    low, high = b * LANES - HALO, (b + 1) * LANES + HALO
    parts = []
    if low < 0:
        parts.append(jnp.where(tile == 0, 0.0, edge()))
    parts.append(own(max(low, 0), min(high, size)))
    if high > size:
        parts.append(jnp.where(tile == n_tile - 1, 0.0, edge()))
    return jnp.concatenate(parts, axis=0)


def science_kernel(n_tile, sci, edge, lrow, wcol, after, *refs):
    count = len(refs) // 2 - 1
    d0, mid, sems = refs[count], refs[-2], refs[-1]
    copies = [pltpu.make_async_copy(refs[i], refs[count + 1 + i], sems.at[i]) for i in range(count)]
    for copy in copies:
        copy.start()
    tile = lax.axis_index("tile")
    nblk, rows = sci.shape[:2]
    nrow = rows // LANES
    for b in range(nrow):
        left = lrow[variant(tile, b, n_tile, nrow)]
        for m in range(0, nblk, 2):

            def own(lo, hi):
                return jnp.concatenate([sci[m, lo:hi, :], sci[m + 1, lo:hi, :]], axis=1)

            x = window_rows(tile, b, n_tile, nrow, own, lambda: edge[:, m * LANES : (m + 2) * LANES])
            y = dot(left, stack3(x))
            mid[m, b * LANES : (b + 1) * LANES, :] = y[:, :LANES]
            mid[m + 1, b * LANES : (b + 1) * LANES, :] = y[:, LANES:]
    lane = lane_index((rows, LANES))
    for m in range(nblk):
        v = 0 if m == 0 else (2 if m == nblk - 1 else 1)
        rim = jnp.where(lane < 64, mid[min(m + 1, nblk - 1)], mid[max(m - 1, 0)])
        hi, lo = split(jnp.concatenate([mid[m], rim], axis=1))
        d0[:, m * LANES : (m + 1) * LANES] = dot(hi, wcol[v, 0]) + dot(lo, wcol[v, 0]) + dot(hi, wcol[v, 1])
    for copy in copies:
        copy.wait()


def load_kernel(n_tile, *refs):
    half = len(refs) // 2
    after, sci, flags, lrow, *tables = refs[:half]
    sb, fb, lout, *outs = refs[half:-1]
    sems = refs[-1]
    tile = lax.axis_index("tile")
    nblk, rows = sb.shape[:2]
    nrow = rows // LANES
    pairs = []
    for m in range(nblk):
        piece = slice(m * LANES, (m + 1) * LANES)
        pairs += [(sci.at[:, piece], sb.at[m]), (flags.at[:, piece], fb.at[m])]
    pairs += [(lrow.at[variant(tile, b, n_tile, nrow)], lout.at[b]) for b in range(nrow)]
    pairs += list(zip(tables, outs))
    copies = [pltpu.make_async_copy(a, b, sems.at[i]) for i, (a, b) in enumerate(pairs)]
    for copy in copies:
        copy.start()
    for copy in copies:
        copy.wait()


def cut_kernel(info, sb, fb, after, wp, sp, places):
    stamps = info.shape[0] // 2
    nblk = sb.shape[0]
    for i in range(2 * stamps):
        places[i] = info[i]
    lane = lane_index((STAMP, LANES))
    for g in range(stamps // 4):
        w = jnp.zeros((STAMP, LANES), F32)
        s = jnp.zeros((STAMP, LANES), F32)
        for q in range(4):
            top = info[g * 4 + q]
            left = info[stamps + g * 4 + q]
            blk = left // LANES
            off = left - blk * LANES
            nxt = jnp.minimum(blk + 1, nblk - 1)
            shift = lax.rem(q * STAMP - off + LANES, LANES)
            near = lane < q * STAMP - off + LANES
            here = (lane >= q * STAMP) & (lane < (q + 1) * STAMP)

            def window(ref):
                a = pltpu.roll(ref[blk, pl.ds(top, STAMP), :], shift, 1)
                b = pltpu.roll(ref[nxt, pl.ds(top, STAMP), :], shift, 1)
                return jnp.where(near, a, b)

            w = jnp.where(here & (window(fb) == 0), 1.0, w)
            s = jnp.where(here, window(sb), s)
        wp[g * STAMP : (g + 1) * STAMP, :] = w
        sp[g * STAMP : (g + 1) * STAMP, :] = jnp.where(w > 0.0, s, 0.0)


def put_block(n_tile, block, at, t):
    tile = lax.axis_index("tile")
    rows = block.shape[0] - HALO
    e = block[rows:, :]
    t[at + 1, 0:HALO, :] = jnp.where(tile == 0, 0.0, e)
    t[at + 1, HALO : HALO + rows, :] = block[0:rows, :]
    t[at + 1, HALO + rows :, :] = jnp.where(tile == n_tile - 1, 0.0, e)


def stamp_kernel(n_tile, nblk, ring, info, last, t_in, wp, sp, mcol, after, system, t, y, images):
    stamps = info.shape[0] // 2
    put_block(n_tile, last, slot_block(nblk - 1, nblk, ring), t)
    groups = stamps // 4
    lane = lane_index((PATCH_ROWS, LANES))
    prof = profiles()
    xs = []
    for g in range(groups):
        halves = []
        for pair in range(2):
            parts = []
            for h in range(2):
                j = g * 4 + pair * 2 + h
                start = info[stamps + j] + (LANES - HALF)
                blk = start // LANES
                off = start - blk * LANES
                shift = lax.rem(64 * h - off + LANES, LANES)
                rows = pl.ds(info[j] + (HALO - HALF), PATCH_ROWS)
                a = pltpu.roll(t[blk, rows, :], shift, 1)
                b = pltpu.roll(t[blk + 1, rows, :], shift, 1)
                parts.append(jnp.where(lane < 64 * h - off + LANES, a, b))
            halves.append(jnp.where(lane < 64, parts[0], parts[1]))
        xs.append(jnp.concatenate(halves, axis=1))
    hi, lo = split(jnp.concatenate(xs, axis=0))
    both = jnp.concatenate([hi, lo], axis=0)
    depth = groups * PATCH_ROWS
    for p in range(0, 6, 2):
        piece = slice(p * LANES, (p + 2) * LANES)
        main = dot(both, mcol[0, :, piece])
        total = main[:depth] + main[depth:] + dot(hi, mcol[1, :, piece])
        y[p] = total[:, :LANES]
        y[p + 1] = total[:, LANES:]
    for s in range(3):
        gauss = prof[2 * s]
        for j in range(2):
            for g in range(groups):
                base = g * PATCH_ROWS

                def at(o):
                    return y[2 * s + j, base + HALF + o : base + HALF + o + STAMP, :]

                even = at(0) * np.float32(gauss[HALF])
                odd = None
                for d in range(1, HALF + 1):
                    up, down = at(d), at(-d)
                    even = even + (up + down) * np.float32(gauss[HALF + d])
                    term = (up - down) * np.float32(gauss[HALF + d] * d / HALF)
                    odd = term if odd is None else odd + term
                images[4 * s + 2 * j, g * STAMP : (g + 1) * STAMP, :] = even
                images[4 * s + 2 * j + 1, g * STAMP : (g + 1) * STAMP, :] = odd
    depth = groups * STAMP
    row = row_index((8, LANES))
    lane = lane_index((8, LANES))
    zero = jnp.zeros((8, LANES), F32)
    tiles = [[zero, zero] for _ in range(NB + 1)]

    def collect(k, l, x):
        tiles[l][k // 8] = jnp.where(row == k % 8, x, tiles[l][k // 8])

    w = wp[...]
    for k in range(NB):
        weighted = w * images[k]
        for l in range(k, NB + 1):
            prod = weighted * images[l] if l < NB else sp[...] * images[k]
            x = jnp.sum(prod.reshape(depth // 8, 8, LANES), axis=0)
            for d in (4, 2, 1):
                x = x + pltpu.roll(x, d, 0)
            collect(k, l, x)
            if k < l < NB:
                collect(l, k, x)
    for h in range(2):
        out = zero
        for l in range(NB + 1):
            out = jnp.where(lane == l, jnp.sum(tiles[l][h], axis=1, keepdims=True), out)
        system[h * 8 : (h + 1) * 8, :] = out


def rows_kernel(n_tile, slots, ring, store, lrow, after, *refs):
    blocks = refs[: len(slots)]
    rhi, rlo = refs[-3:-1] if store else refs[-2:]
    tile = lax.axis_index("tile")
    nblk, _, rows = rhi.shape[:3]
    nrow = rows // LANES
    places = [slot_block(slot, nblk, ring) for slot in slots]
    if store:
        t = refs[-1]
        if slots[0] == 0:
            t[0] = jnp.zeros(t.shape[1:], F32)
            t[nblk + 1] = jnp.zeros(t.shape[1:], F32)
        for block, at in zip(blocks, places):
            put_block(n_tile, block, at, t)
    for b in range(nrow):
        xs = [
            window_rows(tile, b, n_tile, nrow, lambda lo, hi: block[lo:hi, :], lambda: block[rows:, :])
            for block in blocks
        ]
        hi, lo = split(dot(lrow[b], stack3(jnp.concatenate(xs, axis=1) if len(xs) > 1 else xs[0])))
        for h, at in enumerate(places):
            for p in range(6):
                piece = (slice(p * LANES, (p + 1) * LANES), slice(h * LANES, (h + 1) * LANES))
                rhi[at, p, b * LANES : (b + 1) * LANES, :] = hi[piece]
                rlo[at, p, b * LANES : (b + 1) * LANES, :] = lo[piece]


def columns_kernel(nblk, places, ring, rhi, rlo, wcol, after, *refs):
    out = refs[-1]
    rows = rhi.shape[2]
    lane = lane_index((2 * rows, LANES))
    reach = 2 * HALF
    in_low = (lane >= 96 - reach) & (lane < 96 + reach)
    in_high = (lane >= 64 - reach) & (lane < 64 + reach)
    for place in places:
        m = place_block(place, nblk, ring)
        v = jnp.where(m == 0, 0, jnp.where(m == nblk - 1, 2, 1))
        after = jnp.minimum(m + 1, nblk - 1)
        before = jnp.maximum(m - 1, 0)
        for s in range(3):

            def get(ref, i):
                return ref[i, 2 * s : 2 * s + 2].reshape(2 * rows, LANES)

            def rim(ref):
                return jnp.where(lane < 64, get(ref, after), get(ref, before))

            high, low, own = rim(rhi), rim(rlo), get(rhi, m)
            packed = jnp.where(in_low, pltpu.roll(low, 96, 1), jnp.where(in_high, pltpu.roll(high, 64, 1), high))
            q = dot(jnp.concatenate([own, get(rlo, m)], axis=1), wcol[v, s, 0])
            q = q + dot(jnp.concatenate([own, packed], axis=1), wcol[v, s, 1])
            for i in range(2):
                for j in range(2):
                    out[m, 4 * s + i + 2 * j] = q[i * rows : (i + 1) * rows, j * LANES : (j + 1) * LANES]


def final_kernel(system, d0, images, detection, coefficients, solved, out, scalars, sems):
    a = system[...]
    row = row_index(a.shape)
    col = [jnp.broadcast_to(a[:, j : j + 1], a.shape) for j in range(NB + 1)]
    trace = col[0][0:1, :]
    for k in range(1, NB):
        trace = trace + col[k][k : k + 1, :]
    ridge = trace * (0.05 / NB)
    for k in range(NB):
        col[k] = jnp.where(row == k, col[k] + ridge, col[k])
    result = jnp.zeros(a.shape, F32)
    for k in range(NB):
        factor = jnp.where(row == k, 0.0, col[k] * (1.0 / col[k][k : k + 1, :]))
        for j in range(k + 1, NB + 1):
            col[j] = col[j] - factor * col[j][k : k + 1, :]
    for k in range(NB):
        result = jnp.where(row == k, col[NB] / col[k], result)
    solved[...] = result
    for k in range(NB):
        scalars[k] = solved[k, 0]
    nblk, _, rows = images.shape[:3]
    parts = sems.shape[0] - 1
    size = rows // parts
    copies = [pltpu.make_async_copy(scalars, coefficients, sems.at[parts])]
    copies[0].start()
    for c in range(parts):
        piece = slice(c * size, (c + 1) * size)
        for m in range(nblk):
            total = d0[piece, m * LANES : (m + 1) * LANES]
            for k in range(NB):
                total = total - solved[k : k + 1, :] * images[m, k, piece, :]
            out[piece, m * LANES : (m + 1) * LANES] = total
        copies.append(pltpu.make_async_copy(out.at[piece], detection.at[piece], sems.at[c]))
        copies[-1].start()
    for copy in copies:
        copy.wait()


def ring_order(count):
    return list(range(0, count, 2)) + list(range(count - 1, 0, -2))


def swap(x):
    return lax.ppermute(x, "tile", [(0, 1), (1, 0)])


def gather_ring(block, count):
    ring = ring_order(count)
    ahead = [(ring[i], ring[(i - 1) % count]) for i in range(count)]
    back = [(t, s) for s, t in ahead]
    out = [block]
    fwd = bwd = block
    for step in range(count // 2):
        if step < count // 2 - 1:
            bwd = lax.ppermute(bwd, "epoch", back)
        fwd = lax.ppermute(fwd, "epoch", ahead)
        out += [fwd, bwd]
    return out[:count]


def all_sum(x, count, beside):
    beside[0](x)
    x = x + swap(x)
    if count & (count - 1) or count < 4:
        for f in beside[1:]:
            f(x)
        return lax.psum(x, "epoch")

    def other(bits):
        return lax.ppermute(x, "epoch", [(j, j ^ bits) for j in range(count)])

    beside[1](x)
    x = (x + other(1)) + (other(2) + other(3))
    bit = 4
    for f in beside[2:]:
        f(x)
    while bit < count:
        x = x + other(bit)
        bit *= 2
    return x


def in_vmem(x):
    return pltpu.with_memory_space_constraint(x, pltpu.VMEM)


ANY = functools.partial(pl.BlockSpec, memory_space=pl.ANY)
HBM = functools.partial(pl.BlockSpec, memory_space=pltpu.HBM)


def call(kernel, name, out, ins, limit, flops, scratch=(), aliases=None, outside=(), hbm=()):
    ins = [pltpu.with_memory_space_constraint(x, pltpu.HBM) if i in hbm else x for i, x in enumerate(ins)]

    def spec(i, x):
        if i in outside:
            return ANY()
        if i in hbm:
            return HBM()
        return SMEM() if x.ndim == 1 else VMEM()

    return pl.pallas_call(
        kernel,
        out_shape=out,
        in_specs=[spec(i, x) for i, x in enumerate(ins)],
        out_specs=jax.tree.map(lambda x: SMEM() if len(x.shape) == 1 else VMEM(), out, is_leaf=lambda x: hasattr(x, "shape")),
        scratch_shapes=scratch,
        input_output_aliases=aliases or {},
        compiler_params=pltpu.CompilerParams(vmem_limit_bytes=limit * 2**20),
        cost_estimate=pl.CostEstimate(flops=flops, bytes_accessed=2**20, transcendentals=0),
        name=name,
    )(*ins)


def local(template, science, flags, stamp_rows, stamp_cols):
    n_tile = lax.axis_size("tile")
    n_epoch = lax.axis_size("epoch")
    rows, width = template.shape
    science, flags = science[0], flags[0]
    cols = science.shape[1]
    nblk = cols // LANES
    nrow = rows // LANES
    stamps = stamp_rows.shape[1]
    groups = stamps // 4
    depth = groups * STAMP
    ring = width == LANES
    tile = lax.axis_index("tile")

    def edge_of(x):
        return jnp.where(tile == 0, x[-HALO:], x[:HALO])

    other = swap(template)
    tall = lax.optimization_barrier(jnp.pad(template, ((0, HALO), (0, 0))))
    tall = lax.dynamic_update_slice(tall, jnp.where(tile == 0, other[:HALO], other[-HALO:]), (rows, 0))
    _, later, stamp_rows, stamp_cols = lax.optimization_barrier((tall, science, stamp_rows, stamp_cols))
    science_edge = swap(edge_of(later))
    if ring:
        blocks = gather_ring(tall, n_epoch)
    else:
        whole = lax.all_gather(tall, "epoch", axis=1, tiled=True)
        blocks = [whole[:, m * LANES : (m + 1) * LANES] for m in range(nblk)]
    info = jnp.concatenate([stamp_rows[0], stamp_cols[0]])

    lrow6, lrow1 = (jnp.asarray(x) for x in row_tables())
    wcol6, wcol1 = (jnp.asarray(x) for x in column_tables())
    tables = [lrow1, wcol1]
    later_tables = [wcol6, jnp.asarray(stamp_table())]

    def like(xs):
        return tuple(pltpu.VMEM(x.shape, x.dtype) for x in xs)

    sci, bad, lrow6, lrow1, wcol1 = map(in_vmem, call(
        functools.partial(load_kernel, n_tile),
        "load",
        (
            pltpu.VMEM((nblk, rows, LANES), F32),
            pltpu.VMEM((nblk, rows, LANES), jnp.int32),
            pltpu.VMEM((nrow,) + lrow6.shape[1:], BF16),
        )
        + like(tables),
        [tall, science, flags, lrow6] + tables,
        2,
        2 * 10**9,
        [pltpu.SemaphoreType.DMA((2 * nblk + nrow + len(tables),))],
        outside=(0,),
        hbm=range(1, 4 + len(tables)),
    ))
    d0, wcol6, mcol = map(in_vmem, call(
        functools.partial(science_kernel, n_tile),
        "science_filter",
        (pltpu.VMEM((rows, cols), F32),) + like(later_tables),
        [sci, science_edge, lrow1, wcol1, blocks[1]] + later_tables,
        12,
        2 * 10**9,
        [pltpu.VMEM((nblk, rows, LANES), F32), pltpu.SemaphoreType.DMA((len(later_tables),))],
        outside=(4,),
        hbm=range(5, 5 + len(later_tables)),
    ))
    wp, sp, info = call(
        cut_kernel,
        "stamp_pixels",
        (pltpu.VMEM((depth, LANES), F32),) * 2 + (pltpu.SMEM(info.shape, info.dtype),),
        [info, sci, bad, blocks[3]],
        4,
        10**9,
        outside=(3,),
    )
    wp, sp = in_vmem(wp), in_vmem(sp)
    info = pltpu.with_memory_space_constraint(info, pltpu.SMEM)

    def row_filters(slots, r, store):
        ins = [lrow6, blocks[1] if store else d0] + [blocks[slot] for slot in slots]
        n = len(ins)
        out = (pltpu.VMEM((nblk, 6, rows, LANES), BF16),) * 2
        if store:
            out += (pltpu.VMEM((nblk + 2, rows + 2 * HALO, LANES), F32),)
        return call(
            functools.partial(rows_kernel, n_tile, slots, ring, store),
            "template_rows",
            out,
            ins + [in_vmem(x) for x in r],
            12,
            10**9,
            aliases={n + i: i for i in range(len(r))},
            outside=(1,),
        )

    def column_filters(places, r, q, after):
        ins = [in_vmem(x) for x in r] + [wcol6, after] + [in_vmem(x) for x in q]
        return call(
            functools.partial(columns_kernel, nblk, places, ring),
            "template_columns",
            pltpu.VMEM((nblk, NB, rows, LANES), F32),
            ins,
            12,
            5 * 10**7 * len(places),
            aliases={4: 0} if q else None,
            outside=(3,),
        )

    r = ()
    for slots in [(0,)] + [(i, i + 1) for i in range(1, nblk - 1, 2)]:
        r = row_filters(slots, r, True)
    padded = r[2]
    state = dict(r=r[:2], q=())

    def more_columns(places):
        def go(x):
            state["q"] = (column_filters(places, state["r"], state["q"], x),)

        return go

    def last_rows(x):
        state["r"] = row_filters((nblk - 1,), state["r"], False)

    more_columns(range(nblk - 4))(blocks[-2])

    system, _ = call(
        functools.partial(stamp_kernel, n_tile, nblk, ring),
        "stamp_sums",
        (pltpu.VMEM((16, LANES), F32), pltpu.VMEM(padded.shape, F32)),
        [info, blocks[-1], in_vmem(padded), wp, sp, mcol, in_vmem(state["q"][0])],
        12,
        10**9,
        [
            pltpu.VMEM((6, groups * PATCH_ROWS, LANES), F32),
            pltpu.VMEM((NB, depth, LANES), F32),
        ],
        aliases={2: 1},
        outside=(6,),
    )
    beside = [last_rows] + [more_columns(range(i, i + 2)) for i in range(nblk - 4, nblk, 2)]
    system = all_sum(system, n_epoch, beside)

    parts = 8
    detection, coefficients = pl.pallas_call(
        final_kernel,
        out_shape=(
            jax.ShapeDtypeStruct((rows, cols), F32),
            jax.ShapeDtypeStruct((NB,), F32),
        ),
        in_specs=[VMEM()] * 3,
        out_specs=(HBM(), HBM()),
        scratch_shapes=[
            pltpu.VMEM((16, LANES), F32),
            pltpu.VMEM((rows, cols), F32),
            pltpu.SMEM((NB,), F32),
            pltpu.SemaphoreType.DMA((parts + 1,)),
        ],
        compiler_params=pltpu.CompilerParams(vmem_limit_bytes=8 * 2**20),
        cost_estimate=pl.CostEstimate(flops=10**8, bytes_accessed=16 * 2**20, transcendentals=0),
        name="solve_subtract",
    )(system, d0, in_vmem(state["q"][0]))
    return (detection[None], coefficients)


def solution(mesh):
    return jax.shard_map(
        local,
        mesh=mesh,
        in_specs=(
            P(("patch", "tile"), "epoch"),
            P(("patch", "epoch"), "tile", None),
            P(("patch", "epoch"), "tile", None),
            P(("patch", "epoch"), "tile"),
            P(("patch", "epoch"), "tile"),
        ),
        out_specs=(P(("patch", "epoch"), "tile", None), P("patch")),
        check_vma=False,
    )
```

```python
import functools

import jax
import jax.numpy as jnp
import numpy as np
from jax import lax
from jax.experimental import pallas as pl
from jax.experimental.pallas import tpu as pltpu
from jax.sharding import PartitionSpec as P

STAMP = 32
HALF = 7
TAPS = 15
SIGMAS = (1.0, 2.0, 3.5)
NB = 12
LANES = 128
HALO = 16
WIN = LANES + 2 * HALO
PATCH_ROWS = 48
F32 = jnp.float32
BF16 = jnp.bfloat16
LIMIT = 56 * 1024 * 1024


def split_np(a):
    a = np.asarray(a, np.float32)
    hi = a.astype(BF16)
    lo = (a - hi.astype(np.float32)).astype(BF16)
    return hi, lo


def profiles():
    offsets = np.arange(TAPS, dtype=np.float64) - HALF
    rows = []
    for sigma in SIGMAS:
        gauss = np.exp(-offsets * offsets / (2.0 * sigma * sigma))
        gauss = gauss / gauss.sum()
        rows += [gauss, gauss * offsets / HALF]
    return np.stack(rows)


def psf_profile():
    offsets = np.arange(TAPS, dtype=np.float64) - HALF
    gauss = np.exp(-offsets * offsets / 4.5)
    return gauss / gauss.sum()


def band(profile, size):
    out = np.zeros((size, size))
    for shift in range(TAPS):
        out += profile[shift] * np.eye(size, k=shift - HALF)
    return out


def three_bands(size):
    psf = band(psf_profile(), size)
    return [psf @ band(p, size) for p in profiles()], psf


def pick(matrix, rows, cols):
    cols = np.asarray(cols)
    ok = (cols >= 0) & (cols < matrix.shape[1])
    out = matrix[np.asarray(rows)[:, None], np.clip(cols, 0, matrix.shape[1] - 1)[None, :]]
    return np.where(ok[None, :], out, 0.0)


def starts():
    return (0, LANES, 2 * LANES)


def row_tables():
    size = 3 * LANES
    ops, psf = three_bands(size)

    def stack(ms):
        out = []
        for start in starts():
            rows = np.arange(LANES) + start
            cols = np.arange(WIN) + start - HALO
            hi, lo = split_np(np.concatenate([pick(m, rows, cols) for m in ms], axis=0))
            out.append(np.concatenate([hi, hi, lo], axis=1))
        return np.stack(out)

    return stack(ops), stack([psf])


def column_tables():
    size = 3 * LANES
    ops, psf = three_bands(size)
    lane = np.arange(LANES)

    def own(matrix, start):
        return split_np(pick(matrix, lane + start, lane + start).T)

    def rim(matrix, start):
        side = np.where(lane < 64, start + LANES + lane, start - LANES + lane)
        return split_np(pick(matrix, lane + start, side).T)

    def model(matrix, start):
        hi, lo = own(matrix, start)
        rhi, rlo = rim(matrix, start)
        packed = np.zeros_like(rhi)
        for at in list(range(2 * HALF)) + list(range(LANES - 2 * HALF, LANES)):
            packed[at] = rhi[at]
            packed[(at + 64) % LANES] = rlo[at]
            packed[(at + 96) % LANES] = rhi[at]
        return np.stack([np.concatenate([hi, hi]), np.concatenate([lo, packed])])

    def science(start):
        return np.stack([np.concatenate(p) for p in zip(own(psf, start), rim(psf, start))])

    models = [
        [np.concatenate([model(ops[2 * s], start), model(ops[2 * s + 1], start)], axis=2) for s in range(3)]
        for start in starts()
    ]
    return np.array(models), np.stack([science(start) for start in starts()])


def stamp_table():
    prof = profiles()
    out = np.zeros((256, 6, LANES))
    for q in range(4):
        for c in range(STAMP):
            for v in range(TAPS):
                out[q * 64 + c + v, :, q * STAMP + c] = prof[:, v]
    return np.stack(split_np(out.reshape(256, 6 * LANES)))


def dot(a, b):
    return jnp.dot(a, b, preferred_element_type=F32)


def split(x):
    hi = x.astype(BF16)
    lo = (x - hi.astype(F32)).astype(BF16)
    return hi, lo


def stack3(x):
    hi, lo = split(x)
    return jnp.concatenate([hi, lo, hi], axis=0)


def params(**kw):
    return pltpu.CompilerParams(vmem_limit_bytes=LIMIT, **kw)


VMEM = functools.partial(pl.BlockSpec, memory_space=pltpu.VMEM)
SMEM = functools.partial(pl.BlockSpec, memory_space=pltpu.SMEM)


def row_index(shape):
    return lax.broadcasted_iota(jnp.int32, shape, len(shape) - 2)


def lane_index(shape):
    return lax.broadcasted_iota(jnp.int32, shape, len(shape) - 1)


def ring_place(step, count):
    me = lax.axis_index("epoch")
    at = jnp.where(lax.rem(me, 2) == 0, me // 2, count - 1 - me // 2)
    at = lax.rem(at + step + count, count)
    return jnp.where(at < count // 2, 2 * at, 2 * (count - 1 - at) + 1)


def slot_block(slot, nblk, ring):
    if not ring:
        return jnp.int32(slot)
    step = (slot + 1) // 2
    return ring_place(-step if slot % 2 == 0 else step, nblk)


def place_block(place, nblk, ring):
    return lax.rem(slot_block(nblk - 1, nblk, ring) + 2 + place, nblk)


def variant(tile, b, n_tile, nrow):
    v = jnp.int32(1)
    if b == 0:
        v = jnp.where(tile == 0, 0, v)
    if b == nrow - 1:
        v = jnp.where(tile == n_tile - 1, 2, v)
    return v


def window_rows(tile, b, n_tile, nrow, own, edge):
    size = nrow * LANES
    low, high = b * LANES - HALO, (b + 1) * LANES + HALO
    parts = []
    if low < 0:
        parts.append(jnp.where(tile == 0, 0.0, edge()))
    parts.append(own(max(low, 0), min(high, size)))
    if high > size:
        parts.append(jnp.where(tile == n_tile - 1, 0.0, edge()))
    return jnp.concatenate(parts, axis=0)


def science_kernel(n_tile, sci, edge, lrow, wcol, after, *refs):
    count = len(refs) // 2 - 1
    d0, mid, sems = refs[count], refs[-2], refs[-1]
    copies = [pltpu.make_async_copy(refs[i], refs[count + 1 + i], sems.at[i]) for i in range(count)]
    for copy in copies:
        copy.start()
    tile = lax.axis_index("tile")
    nblk, rows = sci.shape[:2]
    nrow = rows // LANES
    for b in range(nrow):
        left = lrow[variant(tile, b, n_tile, nrow)]
        for m in range(0, nblk, 2):

            def own(lo, hi):
                return jnp.concatenate([sci[m, lo:hi, :], sci[m + 1, lo:hi, :]], axis=1)

            x = window_rows(tile, b, n_tile, nrow, own, lambda: edge[:, m * LANES : (m + 2) * LANES])
            y = dot(left, stack3(x))
            mid[m, b * LANES : (b + 1) * LANES, :] = y[:, :LANES]
            mid[m + 1, b * LANES : (b + 1) * LANES, :] = y[:, LANES:]
    lane = lane_index((rows, LANES))
    for m in range(nblk):
        v = 0 if m == 0 else (2 if m == nblk - 1 else 1)
        rim = jnp.where(lane < 64, mid[min(m + 1, nblk - 1)], mid[max(m - 1, 0)])
        hi, lo = split(jnp.concatenate([mid[m], rim], axis=1))
        d0[:, m * LANES : (m + 1) * LANES] = dot(hi, wcol[v, 0]) + dot(lo, wcol[v, 0]) + dot(hi, wcol[v, 1])
    for copy in copies:
        copy.wait()


def load_kernel(n_tile, *refs):
    half = len(refs) // 2
    after, sci, flags, lrow, *tables = refs[:half]
    sb, fb, lout, *outs = refs[half:-1]
    sems = refs[-1]
    tile = lax.axis_index("tile")
    nblk, rows = sb.shape[:2]
    nrow = rows // LANES
    pairs = []
    for m in range(nblk):
        piece = slice(m * LANES, (m + 1) * LANES)
        pairs += [(sci.at[:, piece], sb.at[m]), (flags.at[:, piece], fb.at[m])]
    pairs += [(lrow.at[variant(tile, b, n_tile, nrow)], lout.at[b]) for b in range(nrow)]
    pairs += list(zip(tables, outs))
    copies = [pltpu.make_async_copy(a, b, sems.at[i]) for i, (a, b) in enumerate(pairs)]
    for copy in copies:
        copy.start()
    for copy in copies:
        copy.wait()


def cut_kernel(info, sb, fb, after, wp, sp, places):
    stamps = info.shape[0] // 2
    nblk = sb.shape[0]
    for i in range(2 * stamps):
        places[i] = info[i]
    lane = lane_index((STAMP, LANES))
    for g in range(stamps // 4):
        w = jnp.zeros((STAMP, LANES), F32)
        s = jnp.zeros((STAMP, LANES), F32)
        for q in range(4):
            top = info[g * 4 + q]
            left = info[stamps + g * 4 + q]
            blk = left // LANES
            off = left - blk * LANES
            nxt = jnp.minimum(blk + 1, nblk - 1)
            shift = lax.rem(q * STAMP - off + LANES, LANES)
            near = lane < q * STAMP - off + LANES
            here = (lane >= q * STAMP) & (lane < (q + 1) * STAMP)

            def window(ref):
                a = pltpu.roll(ref[blk, pl.ds(top, STAMP), :], shift, 1)
                b = pltpu.roll(ref[nxt, pl.ds(top, STAMP), :], shift, 1)
                return jnp.where(near, a, b)

            w = jnp.where(here & (window(fb) == 0), 1.0, w)
            s = jnp.where(here, window(sb), s)
        wp[g * STAMP : (g + 1) * STAMP, :] = w
        sp[g * STAMP : (g + 1) * STAMP, :] = jnp.where(w > 0.0, s, 0.0)


def put_block(n_tile, block, at, t):
    tile = lax.axis_index("tile")
    rows = block.shape[0] - HALO
    e = block[rows:, :]
    t[at + 1, 0:HALO, :] = jnp.where(tile == 0, 0.0, e)
    t[at + 1, HALO : HALO + rows, :] = block[0:rows, :]
    t[at + 1, HALO + rows :, :] = jnp.where(tile == n_tile - 1, 0.0, e)


def stamp_kernel(n_tile, nblk, ring, info, last, t_in, wp, sp, mcol, after, system, t, y, images):
    stamps = info.shape[0] // 2
    put_block(n_tile, last, slot_block(nblk - 1, nblk, ring), t)
    groups = stamps // 4
    lane = lane_index((PATCH_ROWS, LANES))
    prof = profiles()
    xs = []
    for g in range(groups):
        halves = []
        for pair in range(2):
            parts = []
            for h in range(2):
                j = g * 4 + pair * 2 + h
                start = info[stamps + j] + (LANES - HALF)
                blk = start // LANES
                off = start - blk * LANES
                shift = lax.rem(64 * h - off + LANES, LANES)
                rows = pl.ds(info[j] + (HALO - HALF), PATCH_ROWS)
                a = pltpu.roll(t[blk, rows, :], shift, 1)
                b = pltpu.roll(t[blk + 1, rows, :], shift, 1)
                parts.append(jnp.where(lane < 64 * h - off + LANES, a, b))
            halves.append(jnp.where(lane < 64, parts[0], parts[1]))
        xs.append(jnp.concatenate(halves, axis=1))
    hi, lo = split(jnp.concatenate(xs, axis=0))
    both = jnp.concatenate([hi, lo], axis=0)
    depth = groups * PATCH_ROWS
    for p in range(0, 6, 2):
        piece = slice(p * LANES, (p + 2) * LANES)
        main = dot(both, mcol[0, :, piece])
        total = main[:depth] + main[depth:] + dot(hi, mcol[1, :, piece])
        y[p] = total[:, :LANES]
        y[p + 1] = total[:, LANES:]
    for s in range(3):
        gauss = prof[2 * s]
        for j in range(2):
            for g in range(groups):
                base = g * PATCH_ROWS

                def at(o):
                    return y[2 * s + j, base + HALF + o : base + HALF + o + STAMP, :]

                even = at(0) * np.float32(gauss[HALF])
                odd = None
                for d in range(1, HALF + 1):
                    up, down = at(d), at(-d)
                    even = even + (up + down) * np.float32(gauss[HALF + d])
                    term = (up - down) * np.float32(gauss[HALF + d] * d / HALF)
                    odd = term if odd is None else odd + term
                images[4 * s + 2 * j, g * STAMP : (g + 1) * STAMP, :] = even
                images[4 * s + 2 * j + 1, g * STAMP : (g + 1) * STAMP, :] = odd
    depth = groups * STAMP
    row = row_index((8, LANES))
    lane = lane_index((8, LANES))
    zero = jnp.zeros((8, LANES), F32)
    tiles = [[zero, zero] for _ in range(NB + 1)]

    def collect(k, l, x):
        tiles[l][k // 8] = jnp.where(row == k % 8, x, tiles[l][k // 8])

    w = wp[...]
    for k in range(NB):
        weighted = w * images[k]
        for l in range(k, NB + 1):
            prod = weighted * images[l] if l < NB else sp[...] * images[k]
            x = jnp.sum(prod.reshape(depth // 8, 8, LANES), axis=0)
            for d in (4, 2, 1):
                x = x + pltpu.roll(x, d, 0)
            collect(k, l, x)
            if k < l < NB:
                collect(l, k, x)
    for h in range(2):
        out = zero
        for l in range(NB + 1):
            out = jnp.where(lane == l, jnp.sum(tiles[l][h], axis=1, keepdims=True), out)
        system[h * 8 : (h + 1) * 8, :] = out


def rows_kernel(n_tile, slots, ring, store, lrow, after, *refs):
    blocks = refs[: len(slots)]
    rhi, rlo = refs[-3:-1] if store else refs[-2:]
    tile = lax.axis_index("tile")
    nblk, _, rows = rhi.shape[:3]
    nrow = rows // LANES
    places = [slot_block(slot, nblk, ring) for slot in slots]
    if store:
        t = refs[-1]
        if slots[0] == 0:
            t[0] = jnp.zeros(t.shape[1:], F32)
            t[nblk + 1] = jnp.zeros(t.shape[1:], F32)
        for block, at in zip(blocks, places):
            put_block(n_tile, block, at, t)
    for b in range(nrow):
        xs = [
            window_rows(tile, b, n_tile, nrow, lambda lo, hi: block[lo:hi, :], lambda: block[rows:, :])
            for block in blocks
        ]
        hi, lo = split(dot(lrow[b], stack3(jnp.concatenate(xs, axis=1) if len(xs) > 1 else xs[0])))
        for h, at in enumerate(places):
            for p in range(6):
                piece = (slice(p * LANES, (p + 1) * LANES), slice(h * LANES, (h + 1) * LANES))
                rhi[at, p, b * LANES : (b + 1) * LANES, :] = hi[piece]
                rlo[at, p, b * LANES : (b + 1) * LANES, :] = lo[piece]


def columns_kernel(nblk, places, ring, rhi, rlo, wcol, after, *refs):
    out = refs[-1]
    rows = rhi.shape[2]
    lane = lane_index((2 * rows, LANES))
    reach = 2 * HALF
    in_low = (lane >= 96 - reach) & (lane < 96 + reach)
    in_high = (lane >= 64 - reach) & (lane < 64 + reach)
    for place in places:
        m = place_block(place, nblk, ring)
        v = jnp.where(m == 0, 0, jnp.where(m == nblk - 1, 2, 1))
        after = jnp.minimum(m + 1, nblk - 1)
        before = jnp.maximum(m - 1, 0)
        for s in range(3):

            def get(ref, i):
                return ref[i, 2 * s : 2 * s + 2].reshape(2 * rows, LANES)

            def rim(ref):
                return jnp.where(lane < 64, get(ref, after), get(ref, before))

            high, low, own = rim(rhi), rim(rlo), get(rhi, m)
            packed = jnp.where(in_low, pltpu.roll(low, 96, 1), jnp.where(in_high, pltpu.roll(high, 64, 1), high))
            q = dot(jnp.concatenate([own, get(rlo, m)], axis=1), wcol[v, s, 0])
            q = q + dot(jnp.concatenate([own, packed], axis=1), wcol[v, s, 1])
            for i in range(2):
                for j in range(2):
                    out[m, 4 * s + i + 2 * j] = q[i * rows : (i + 1) * rows, j * LANES : (j + 1) * LANES]


def final_kernel(system, d0, images, detection, coefficients, solved, out, scalars, sems):
    a = system[...]
    row = row_index(a.shape)
    col = [jnp.broadcast_to(a[:, j : j + 1], a.shape) for j in range(NB + 1)]
    trace = col[0][0:1, :]
    for k in range(1, NB):
        trace = trace + col[k][k : k + 1, :]
    ridge = trace * (0.05 / NB)
    for k in range(NB):
        col[k] = jnp.where(row == k, col[k] + ridge, col[k])
    result = jnp.zeros(a.shape, F32)
    for k in range(NB):
        factor = jnp.where(row == k, 0.0, col[k] * (1.0 / col[k][k : k + 1, :]))
        for j in range(k + 1, NB + 1):
            col[j] = col[j] - factor * col[j][k : k + 1, :]
    for k in range(NB):
        result = jnp.where(row == k, col[NB] / col[k], result)
    solved[...] = result
    for k in range(NB):
        scalars[k] = solved[k, 0]
    nblk, _, rows = images.shape[:3]
    parts = sems.shape[0] - 1
    size = rows // parts
    copies = [pltpu.make_async_copy(scalars, coefficients, sems.at[parts])]
    copies[0].start()
    for c in range(parts):
        piece = slice(c * size, (c + 1) * size)
        for m in range(nblk):
            total = d0[piece, m * LANES : (m + 1) * LANES]
            for k in range(NB):
                total = total - solved[k : k + 1, :] * images[m, k, piece, :]
            out[piece, m * LANES : (m + 1) * LANES] = total
        copies.append(pltpu.make_async_copy(out.at[piece], detection.at[piece], sems.at[c]))
        copies[-1].start()
    for copy in copies:
        copy.wait()


def ring_order(count):
    return list(range(0, count, 2)) + list(range(count - 1, 0, -2))


def swap(x):
    return lax.ppermute(x, "tile", [(0, 1), (1, 0)])


def gather_ring(block, count):
    ring = ring_order(count)
    ahead = [(ring[i], ring[(i - 1) % count]) for i in range(count)]
    back = [(t, s) for s, t in ahead]
    out = [block]
    fwd = bwd = block
    for step in range(count // 2):
        if step < count // 2 - 1:
            bwd = lax.ppermute(bwd, "epoch", back)
        fwd = lax.ppermute(fwd, "epoch", ahead)
        out += [fwd, bwd]
    return out[:count]


def all_sum(x, count, beside):
    beside[0](x)
    x = x + swap(x)
    if count & (count - 1) or count < 4:
        for f in beside[1:]:
            f(x)
        return lax.psum(x, "epoch")

    def other(bits):
        return lax.ppermute(x, "epoch", [(j, j ^ bits) for j in range(count)])

    for f in beside[1:2]:
        f(x)
    bit = 4
    while bit < count:
        x = x + other(bit)
        bit *= 2
    for f in beside[2:]:
        f(x)
    x = (x + other(1)) + (other(2) + other(3))
    return x


def in_vmem(x):
    return pltpu.with_memory_space_constraint(x, pltpu.VMEM)


ANY = functools.partial(pl.BlockSpec, memory_space=pl.ANY)
HBM = functools.partial(pl.BlockSpec, memory_space=pltpu.HBM)


def call(kernel, name, out, ins, limit, flops, scratch=(), aliases=None, outside=(), hbm=()):
    ins = [pltpu.with_memory_space_constraint(x, pltpu.HBM) if i in hbm else x for i, x in enumerate(ins)]

    def spec(i, x):
        if i in outside:
            return ANY()
        if i in hbm:
            return HBM()
        return SMEM() if x.ndim == 1 else VMEM()

    return pl.pallas_call(
        kernel,
        out_shape=out,
        in_specs=[spec(i, x) for i, x in enumerate(ins)],
        out_specs=jax.tree.map(lambda x: SMEM() if len(x.shape) == 1 else VMEM(), out, is_leaf=lambda x: hasattr(x, "shape")),
        scratch_shapes=scratch,
        input_output_aliases=aliases or {},
        compiler_params=pltpu.CompilerParams(vmem_limit_bytes=limit * 2**20),
        cost_estimate=pl.CostEstimate(flops=flops, bytes_accessed=2**20, transcendentals=0),
        name=name,
    )(*ins)


def local(template, science, flags, stamp_rows, stamp_cols):
    n_tile = lax.axis_size("tile")
    n_epoch = lax.axis_size("epoch")
    rows, width = template.shape
    science, flags = science[0], flags[0]
    cols = science.shape[1]
    nblk = cols // LANES
    nrow = rows // LANES
    stamps = stamp_rows.shape[1]
    groups = stamps // 4
    depth = groups * STAMP
    ring = width == LANES
    tile = lax.axis_index("tile")

    def edge_of(x):
        return jnp.where(tile == 0, x[-HALO:], x[:HALO])

    other = swap(template)
    tall = lax.optimization_barrier(jnp.pad(template, ((0, HALO), (0, 0))))
    tall = lax.dynamic_update_slice(tall, jnp.where(tile == 0, other[:HALO], other[-HALO:]), (rows, 0))
    _, later, stamp_rows, stamp_cols = lax.optimization_barrier((tall, science, stamp_rows, stamp_cols))
    science_edge = swap(edge_of(later))
    if ring:
        blocks = gather_ring(tall, n_epoch)
    else:
        whole = lax.all_gather(tall, "epoch", axis=1, tiled=True)
        blocks = [whole[:, m * LANES : (m + 1) * LANES] for m in range(nblk)]
    info = jnp.concatenate([stamp_rows[0], stamp_cols[0]])

    lrow6, lrow1 = (jnp.asarray(x) for x in row_tables())
    wcol6, wcol1 = (jnp.asarray(x) for x in column_tables())
    tables = [lrow1, wcol1]
    later_tables = [wcol6, jnp.asarray(stamp_table())]

    def like(xs):
        return tuple(pltpu.VMEM(x.shape, x.dtype) for x in xs)

    sci, bad, lrow6, lrow1, wcol1 = map(in_vmem, call(
        functools.partial(load_kernel, n_tile),
        "load",
        (
            pltpu.VMEM((nblk, rows, LANES), F32),
            pltpu.VMEM((nblk, rows, LANES), jnp.int32),
            pltpu.VMEM((nrow,) + lrow6.shape[1:], BF16),
        )
        + like(tables),
        [tall, science, flags, lrow6] + tables,
        2,
        2 * 10**9,
        [pltpu.SemaphoreType.DMA((2 * nblk + nrow + len(tables),))],
        outside=(0,),
        hbm=range(1, 4 + len(tables)),
    ))
    d0, wcol6, mcol = map(in_vmem, call(
        functools.partial(science_kernel, n_tile),
        "science_filter",
        (pltpu.VMEM((rows, cols), F32),) + like(later_tables),
        [sci, science_edge, lrow1, wcol1, blocks[1]] + later_tables,
        12,
        2 * 10**9,
        [pltpu.VMEM((nblk, rows, LANES), F32), pltpu.SemaphoreType.DMA((len(later_tables),))],
        outside=(4,),
        hbm=range(5, 5 + len(later_tables)),
    ))
    wp, sp, info = call(
        cut_kernel,
        "stamp_pixels",
        (pltpu.VMEM((depth, LANES), F32),) * 2 + (pltpu.SMEM(info.shape, info.dtype),),
        [info, sci, bad, blocks[3]],
        4,
        10**9,
        outside=(3,),
    )
    wp, sp = in_vmem(wp), in_vmem(sp)
    info = pltpu.with_memory_space_constraint(info, pltpu.SMEM)

    def row_filters(slots, r, store):
        ins = [lrow6, blocks[1] if store else d0] + [blocks[slot] for slot in slots]
        n = len(ins)
        out = (pltpu.VMEM((nblk, 6, rows, LANES), BF16),) * 2
        if store:
            out += (pltpu.VMEM((nblk + 2, rows + 2 * HALO, LANES), F32),)
        return call(
            functools.partial(rows_kernel, n_tile, slots, ring, store),
            "template_rows",
            out,
            ins + [in_vmem(x) for x in r],
            12,
            10**9,
            aliases={n + i: i for i in range(len(r))},
            outside=(1,),
        )

    def column_filters(places, r, q, after):
        ins = [in_vmem(x) for x in r] + [wcol6, after] + [in_vmem(x) for x in q]
        return call(
            functools.partial(columns_kernel, nblk, places, ring),
            "template_columns",
            pltpu.VMEM((nblk, NB, rows, LANES), F32),
            ins,
            12,
            5 * 10**7 * len(places),
            aliases={4: 0} if q else None,
            outside=(3,),
        )

    r = ()
    for slots in [(0,)] + [(i, i + 1) for i in range(1, nblk - 1, 2)]:
        r = row_filters(slots, r, True)
    padded = r[2]
    state = dict(r=r[:2], q=())

    def more_columns(places):
        def go(x):
            state["q"] = (column_filters(places, state["r"], state["q"], x),)

        return go

    def last_rows(x):
        state["r"] = row_filters((nblk - 1,), state["r"], False)

    more_columns(range(nblk - 4))(blocks[-2])

    system, _ = call(
        functools.partial(stamp_kernel, n_tile, nblk, ring),
        "stamp_sums",
        (pltpu.VMEM((16, LANES), F32), pltpu.VMEM(padded.shape, F32)),
        [info, blocks[-1], in_vmem(padded), wp, sp, mcol, in_vmem(state["q"][0])],
        12,
        10**9,
        [
            pltpu.VMEM((6, groups * PATCH_ROWS, LANES), F32),
            pltpu.VMEM((NB, depth, LANES), F32),
        ],
        aliases={2: 1},
        outside=(6,),
    )
    beside = [last_rows] + [more_columns(range(i, i + 2)) for i in range(nblk - 4, nblk, 2)]
    system = all_sum(system, n_epoch, beside)

    parts = 8
    detection, coefficients = pl.pallas_call(
        final_kernel,
        out_shape=(
            jax.ShapeDtypeStruct((rows, cols), F32),
            jax.ShapeDtypeStruct((NB,), F32),
        ),
        in_specs=[VMEM()] * 3,
        out_specs=(HBM(), HBM()),
        scratch_shapes=[
            pltpu.VMEM((16, LANES), F32),
            pltpu.VMEM((rows, cols), F32),
            pltpu.SMEM((NB,), F32),
            pltpu.SemaphoreType.DMA((parts + 1,)),
        ],
        compiler_params=pltpu.CompilerParams(vmem_limit_bytes=8 * 2**20),
        cost_estimate=pl.CostEstimate(flops=10**8, bytes_accessed=16 * 2**20, transcendentals=0),
        name="solve_subtract",
    )(system, d0, in_vmem(state["q"][0]))
    return (detection[None], coefficients)


def solution(mesh):
    return jax.shard_map(
        local,
        mesh=mesh,
        in_specs=(
            P(("patch", "tile"), "epoch"),
            P(("patch", "epoch"), "tile", None),
            P(("patch", "epoch"), "tile", None),
            P(("patch", "epoch"), "tile"),
            P(("patch", "epoch"), "tile"),
        ),
        out_specs=(P(("patch", "epoch"), "tile", None), P("patch")),
        check_vma=False,
    )
```
